32 devices in a mesh: dp: 8 (over z, y), tensor: 4 (over x, core).
Axes of the slice: x: 2, y: 2, z: 4, core: 2. Of those that a mesh axis runs over, the one named last changes fastest.
Arguments:
- inputs: bfloat16 [16, 2048, 768], P('dp', 'tensor'), may hold values from -6 to 6
- lengths: int32 [16], P('dp'), may hold values from 256 to 2048, as said below
- w_qkv: bfloat16 [768, 3, 768], P(None, None, 'tensor'), may hold values from -0.21875 to 0.21875
- b_qkv: float32 [3, 768], P(None, 'tensor'), may hold values from -4 to 4
- output_weight: bfloat16 [768, 768], P('tensor'), may hold values from -0.4375 to 0.4375
- b_out: float32 [768], replicated, may hold values from -4 to 4
- length_proj: bfloat16 [2048, 256], replicated, may hold values from -0.375 to 0.375
- first_gain: float32 [768], replicated, may hold values from 0.5 to 1.5
- first_shift: float32 [768], replicated, may hold values from -3 to 3
- w_up: bfloat16 [768, 3072], P('dp', 'tensor'), may hold values from -0.21875 to 0.21875
- hidden_bias: float32 [3072], P('tensor'), may hold values from -4 to 4
- w_down: bfloat16 [768, 3072], P('dp', 'tensor'), may hold values from -0.21875 to 0.21875
- b_down: float32 [768], replicated, may hold values from -4 to 4
- second_gain: float32 [768], replicated, may hold values from 0.5 to 1.5
- second_shift: float32 [768], replicated, may hold values from -3 to 3
- cotangent: bfloat16 [16, 2048, 768], P('dp', 'tensor'), may hold values from -6 to 6
Outputs:
- result: bfloat16 [16, 2048, 768], P('dp', 'tensor')
- grad_inputs: bfloat16 [16, 2048, 768], P('dp', 'tensor')
- grad_w_qkv: float32 [768, 3, 768], P(None, None, 'tensor')
- grad_b_qkv: float32 [3, 768], P(None, 'tensor')
- grad_w_out: float32 [768, 768], P('tensor')
- grad_b_out: float32 [768], replicated
- grad_length_proj: float32 [2048, 256], replicated
- grad_first_gain: float32 [768], replicated
- grad_first_shift: float32 [768], replicated
- up_weight_gradient: float32 [768, 3072], P('dp', 'tensor')
- grad_b_up: float32 [3072], P('tensor')
- down_weight_gradient: float32 [768, 3072], P('dp', 'tensor')
- grad_b_down: float32 [768], replicated
- grad_second_gain: float32 [768], replicated
- grad_second_shift: float32 [768], replicated
The draws below stay inside these ranges and needn't reach their ends.
Inputs may be any that keep to these rules, and one draw needn't show every extreme that they name: `lengths`: of the 2 slots of each index of dp, one is 2048 tokens long; the others hold any length in the range.
All inputs are finite; a program needn't handle non-finite values.
Results may differ from the reference program's by a relative error of at most 0.025.
The reference program's roundings to bfloat16 on the way count: a program that leaves them out, or rounds other values in their place, can miss the bound.
Values may be sent and summed in bfloat16 or wider, within the bound.
No kernel may reach another device: no remote copies, remote signals or barrier semaphores. Data moves between devices by JAX's collectives and lax.ppermute only.
A program may use at most 192 MiB of HBM per device.

```python
import jax
import jax.numpy as jnp
from jax import lax

D = 768
H = 12
DH = 64
FF = 3072
KP = 256
LMAX = 2048
LMIN = 256
SEQ_DEV = 2
SEQS = 16


def draw_lengths(key, part):
    key = jax.random.fold_in(key, 7)
    first_key, second_key = jax.random.split(key)
    groups = SEQS // SEQ_DEV
    spans = jax.random.randint(first_key, (groups, SEQ_DEV), LMIN, LMAX + 1)
    chosen = jax.random.randint(second_key, (groups, 1), 0, SEQ_DEV)
    full_slot = jnp.arange(SEQ_DEV)[None, :] == chosen
    return jnp.where(full_slot, LMAX, spans).reshape(SEQS).astype(jnp.int32)


def block_levels(rng, extent, cuts, least, largest):
    level, own = 1.0, jax.random.fold_in(rng, 6)
    for dim, shards_of in cuts:
        steps = jnp.exp(jax.random.uniform(jax.random.fold_in(own, dim), (shards_of,), jnp.float32, least / len(cuts), largest / len(cuts)))
        level = level * jnp.repeat(steps, extent[dim] // shards_of).reshape([-1 if axis == dim else 1 for axis in range(len(extent))])
    return level


def bell_draw(stream_key, shape, scale, bound, pieces=(), held_as=jnp.bfloat16):
    drawn = scale * jax.random.normal(stream_key, shape, jnp.float32)
    if pieces:
        drawn = drawn * block_levels(stream_key, shape, pieces, -0.22, 0.18)
    return jnp.clip(drawn, -bound, bound).astype(held_as)


def setup_inputs(seed: int = 0) -> dict:
    arg_keys = jax.random.split(jax.random.key(seed), 17)
    inputs = bell_draw(arg_keys[0], (SEQS, LMAX, D), 1.0, 6.0, ((0, 8), (1, 4)))
    lengths = draw_lengths(jax.random.fold_in(arg_keys[16], 71), 0)
    w_qkv = bell_draw(arg_keys[2], (D, 3, D), D ** -0.5, 0.21875, ((2, 4),))
    b_qkv = bell_draw(arg_keys[3], (3, D), 0.3, 4.0, ((1, 4),), jnp.float32)
    output_weight = bell_draw(arg_keys[4], (D, D), (D // 4) ** -0.5, 0.4375, ((0, 4),))
    b_out = bell_draw(arg_keys[5], (D,), 0.3, 4.0, (), jnp.float32)
    length_proj = bell_draw(arg_keys[6], (LMAX, KP), KP ** -0.5, 0.375)
    first_gain = jnp.clip(1.0 + 0.1 * jax.random.normal(arg_keys[7], (D,), jnp.float32), 0.5, 1.5)
    first_shift = bell_draw(arg_keys[8], (D,), 0.2, 3.0, (), jnp.float32)
    w_up = bell_draw(arg_keys[9], (D, FF), D ** -0.5, 0.21875, ((0, 8), (1, 4)))
    hidden_bias = bell_draw(arg_keys[10], (FF,), 0.3, 4.0, ((0, 4),), jnp.float32)
    w_down = bell_draw(arg_keys[11], (D, FF), (FF // 4) ** -0.5, 0.21875, ((0, 8), (1, 4)))
    b_down = bell_draw(arg_keys[12], (D,), 0.3, 4.0, (), jnp.float32)
    second_gain = jnp.clip(1.0 + 0.1 * jax.random.normal(arg_keys[13], (D,), jnp.float32), 0.5, 1.5)
    second_shift = bell_draw(arg_keys[14], (D,), 0.2, 3.0, (), jnp.float32)
    cotangent = bell_draw(arg_keys[15], (SEQS, LMAX, D), 1.0, 6.0, ((0, 8), (1, 4)))
    return dict(inputs=inputs, lengths=lengths, w_qkv=w_qkv, b_qkv=b_qkv, output_weight=output_weight, b_out=b_out, length_proj=length_proj, first_gain=first_gain, first_shift=first_shift, w_up=w_up, hidden_bias=hidden_bias, w_down=w_down, b_down=b_down, second_gain=second_gain, second_shift=second_shift, cotangent=cotangent)


@jax.custom_vjp
def low(v):
    return lax.optimization_barrier(v.astype(jnp.bfloat16)).astype(jnp.float32)

@jax.custom_vjp
def low_back(v):
    return v

def low_keep(v):
    return (low(v), None)

def low_pass(kept, grad):
    return (grad,)

def back_keep(v):
    return (v, None)

def back_low(kept, grad):
    return (low(grad),)
low.defvjp(low_keep, low_pass)
low_back.defvjp(back_keep, back_low)
highest = lax.Precision.HIGHEST
epsilon = 1e-05

def norm_rows(summed, gain, shift):
    center = lax.optimization_barrier(jnp.mean(summed, axis=-1, keepdims=True))
    offsets = summed - center
    spread = lax.optimization_barrier(jnp.mean(offsets * offsets, axis=-1, keepdims=True))
    return offsets * lax.rsqrt(spread + epsilon) * gain + shift

def layer_rows(param_set, sequence, length):
    w_qkv, b_qkv, output_weight, b_out, length_proj, first_gain, first_shift, w_up, hidden_bias, w_down, b_down, second_gain, second_shift = param_set
    query_key_value_rows = jnp.einsum('ld,dte->lte', sequence, w_qkv, precision=highest) + b_qkv
    query_key_value_rows = low(low_back(query_key_value_rows))
    queries = query_key_value_rows[:, 0].reshape(LMAX, H, DH)
    key_rows = query_key_value_rows[:, 1].reshape(LMAX, H, DH)
    value_rows = query_key_value_rows[:, 2].reshape(LMAX, H, DH)
    within = (jnp.arange(LMAX) < length).astype(jnp.float32)
    masked = length_proj * within[:, None]
    key_proj = low(low_back(jnp.einsum('lk,lhd->khd', masked, key_rows, precision=highest)))
    value_proj = low(low_back(jnp.einsum('lk,lhd->khd', masked, value_rows, precision=highest)))
    scores = low_back(jnp.einsum('lhd,khd->hlk', queries, key_proj, precision=highest) * DH ** (-0.5))
    weights = jax.nn.softmax(scores, axis=-1)
    heads_out = jnp.einsum('hlk,khd->lhd', low(weights), value_proj, precision=highest).reshape(LMAX, H * DH)
    heads_out = low(low_back(heads_out))
    branch = low_back(jnp.dot(heads_out, output_weight, precision=highest) + b_out)
    first_norm = norm_rows(sequence + branch, first_gain, first_shift)
    hidden_preactivation = low_back(jnp.dot(low(first_norm), w_up, precision=highest) + hidden_bias)
    hidden_activation = low(jax.nn.gelu(hidden_preactivation, approximate=False))
    ffn_branch = low_back(jnp.dot(hidden_activation, w_down.T, precision=highest) + b_down)
    return norm_rows(first_norm + ffn_branch, second_gain, second_shift)

def reference(inputs, lengths, w_qkv, b_qkv, output_weight, b_out, length_proj, first_gain, first_shift, w_up, hidden_bias, w_down, b_down, second_gain, second_shift, cotangent):
    param_set = tuple((weight.astype(jnp.float32) for weight in (w_qkv, b_qkv, output_weight, b_out, length_proj, first_gain, first_shift, w_up, hidden_bias, w_down, b_down, second_gain, second_shift)))
    inputs_wide = inputs.astype(jnp.float32)

    def forward(params_in, rows_all):

        def one_sequence(packed):
            return jax.checkpoint(layer_rows)(params_in, packed[0], packed[1])
        return lax.map(one_sequence, (rows_all, lengths))
    outputs, pullback = jax.vjp(forward, param_set, inputs_wide)
    within = (jnp.arange(LMAX)[None, :] < lengths[:, None]).astype(jnp.float32)
    grads, grad_inputs = pullback(cotangent.astype(jnp.float32) * within[:, :, None])
    return (outputs.astype(jnp.bfloat16), grad_inputs.astype(jnp.bfloat16), grads[0], grads[1], grads[2], grads[3], grads[4], grads[5], grads[6], grads[7], grads[8], grads[9], grads[10], grads[11], grads[12])
```

```python
import functools

import jax
import jax.numpy as jnp
from jax import lax
from jax.experimental import pallas as pl
from jax.experimental.pallas import tpu as pltpu
from jax.sharding import PartitionSpec as P

DH = 64
SCALE = DH ** (-0.5)
EPS = 1e-05
F32 = jnp.float32
BF16 = jnp.bfloat16
VMEM_BYTES = 58 * 1024 * 1024


def bits_of(size):
    count = size.bit_length() - 1
    assert 1 << count == size
    return [1 << b for b in range(count)]


class Line:
    def __init__(self):
        self.last = None

    def meet(self, *values):
        count = len(values)
        values = lax.optimization_barrier(values if self.last is None else (*values, self.last))
        self.last = values[0]
        return values[0] if count == 1 else values[:count]

    def after(self, value):
        return lax.optimization_barrier((value, self.last))[0]


def swap(value, axis, bit, size):
    return lax.ppermute(value, axis, [(i, i ^ bit) for i in range(size)])


def own_bit(axis, bit):
    return (lax.axis_index(axis) & bit) != 0


def add(a, *more):
    for b in more:
        a = a.astype(F32) + b.astype(F32)
    return a.astype(BF16)


def add_pairs(a, b, c, d):
    a, b, c, d = (v.astype(F32) for v in (a, b, c, d))
    return ((a + b) + (c + d)).astype(BF16)


def norm_stats(rows):
    center = jnp.mean(rows, axis=-1, keepdims=True)
    offsets = rows - center
    rstd = lax.rsqrt(jnp.mean(offsets * offsets, axis=-1, keepdims=True) + EPS)
    return offsets * rstd, rstd


def norm_back(normed, rstd, gain, grad):
    g = grad * gain
    return rstd * (
        g
        - jnp.mean(g, axis=-1, keepdims=True)
        - normed * jnp.mean(g * normed, axis=-1, keepdims=True)
    )


def mm(a, b, ca=1, cb=0):
    return lax.dot_general(a, b, (((ca,), (cb,)), ((), ())), preferred_element_type=F32)


def normal_parts(values):
    bell = jnp.exp(values * values * -0.5)
    inverse = 1.0 / (1.0 + (0.3275911 * 0.7071067811865476) * jnp.abs(values))
    tail = inverse * (
        0.127414796
        + inverse
        * (-0.142248368 + inverse * (0.7107068705 + inverse * (-0.7265760135 + inverse * 0.5307027145)))
    )
    tail = tail * bell
    cumulative = jnp.where(values >= 0, 1.0 - tail, tail)
    return cumulative, cumulative + values * bell * 0.3989422804014327


def project_kernel(seqs, scal_ref, x_ref, here_ref, all_ref, sent_ref, kept_ref, sum_ref):
    step = pl.program_id(0)
    seq = scal_ref[2] ^ 1 ^ step
    length = scal_ref[3 + seq]
    rows, kp = here_ref.shape
    place = scal_ref[1] + lax.broadcasted_iota(jnp.int32, (rows, kp), 0)
    here = here_ref[...]
    masked = jnp.where(place < length, here, jnp.zeros_like(here))
    part = mm(masked, x_ref[0], 0, 0)

    @pl.when(step == 0)
    def _():
        sent_ref[...] = part.astype(BF16)

    @pl.when(step == 1)
    def _():
        kept_ref[...] = part

    place = lax.broadcasted_iota(jnp.int32, all_ref.shape, 0)
    every = all_ref[...]
    masked = jnp.where(place < length, every, jnp.zeros_like(every))
    sum_ref[0] = mm(masked, jnp.ones((all_ref.shape[0], 128), BF16), 0, 0)


def split_pairs(src, dst):
    pairs, kp2, pair_cols = dst.shape
    kp = kp2 // 2
    lane = lax.broadcasted_iota(jnp.int32, (kp, pair_cols), 1) < pair_cols // 2
    for pair in range(pairs):
        both = src[0, :, pair * pair_cols : (pair + 1) * pair_cols]
        zero = jnp.zeros_like(both)
        dst[pair, :kp] = jnp.where(lane, both, zero)
        dst[pair, kp:] = jnp.where(lane, zero, both)


def piece_copies(plan, split, pieces, w, sems):
    cols = pieces[0].shape[1] // 4
    copies = []
    for at, (piece, row, block, kind, turned) in enumerate(plan):
        kind = kind ^ (2 * split) if turned else kind
        copies.append(
            pltpu.make_async_copy(
                pieces[piece].at[pl.ds(row, cols)], w.at[kind, pl.ds(block * cols, cols)], sems.at[at]
            )
        )
    return copies


def attend_kernel(plan, count, scal_ref, x_ref, px0_ref, px1_ref, ks_ref, *rest):
    pieces = rest[:count]
    bias_ref, vec_ref = rest[count : count + 2]
    q_ref, p_ref, kp_ref, vp_ref, heads_ref, n1_ref, nl_ref, r1_ref = rest[count + 2 : count + 10]
    w, kst, vst, sems = rest[count + 10 :]
    step = pl.program_id(0)
    pairs, kp2, pair_cols = kst.shape
    kp = kp2 // 2

    @pl.when(step == 0)
    def _():
        copies = piece_copies(plan, scal_ref[0] & 1, pieces, w, sems)
        for copy in copies:
            copy.start()
        for copy in copies:
            copy.wait()

    px = jnp.where(step == 0, px0_ref[...], px1_ref[...])
    ks = ks_ref[0][:, 0:1]
    kp_ref[0] = (mm(px, w[1], 1, 1) + ks * bias_ref[1:2, :]).astype(BF16)
    vp_ref[0] = (mm(px, w[2], 1, 1) + ks * bias_ref[2:3, :]).astype(BF16)
    split_pairs(kp_ref, kst)
    split_pairs(vp_ref, vst)

    x = x_ref[0]
    q_ref[0] = ((mm(x, w[0], 1, 1) + bias_ref[0:1, :]).astype(BF16) * SCALE).astype(BF16)
    for pair in range(pairs):
        span = slice(pair * pair_cols, (pair + 1) * pair_cols)
        scores = mm(q_ref[0, :, span], kst[pair], 1, 1)
        parts = []
        for side in range(2):
            part = scores[:, side * kp : (side + 1) * kp]
            raised = jnp.exp(part - jnp.max(part, axis=-1, keepdims=True))
            part = raised * (1.0 / jnp.sum(raised, axis=-1, keepdims=True))
            parts.append(part.astype(BF16))
        probs = jnp.concatenate(parts, 1)
        p_ref[0, :, pair * kp2 : (pair + 1) * kp2] = probs
        heads_ref[0, :, span] = mm(probs, vst[pair]).astype(BF16)
    resid = x.astype(F32) + mm(heads_ref[0], w[3]) + vec_ref[5:6, :]
    normed, rstd = norm_stats(resid)
    n1_ref[0] = normed.astype(BF16)
    nl_ref[0] = (normed * vec_ref[0:1, :] + vec_ref[1:2, :]).astype(BF16)
    r1_ref[0] = jnp.broadcast_to(rstd, r1_ref.shape[1:])


def weight_copies(plan, dp_index, pieces, dst, sems, r):
    rows = sum(ref.shape[0] for ref in pieces) // len(plan)
    copies = []
    for at, (piece, row, block, rel) in enumerate(plan):
        if block == r:
            place = pl.multiple_of((dp_index ^ rel) * rows, rows)
            copies.append(
                pltpu.make_async_copy(
                    pieces[piece].at[pl.ds(row, rows)], dst.at[r, pl.ds(place, rows)], sems.at[at]
                )
            )
    return copies


def fetch_weights(dp_index, groups, nt, extra=()):
    step = pl.program_id(0)

    @pl.when(step == 0)
    def _():
        for r in range(nt):
            for plan, pieces, dst, sems in groups:
                for copy in weight_copies(plan, dp_index, pieces, dst, sems, r):
                    copy.start()
        for copy in extra:
            copy.start()

    for r in range(nt):

        @pl.when(step == r)
        def _():
            for plan, pieces, dst, sems in groups:
                for copy in weight_copies(plan, dp_index, pieces, dst, sems, r):
                    copy.wait()


def lay_rows(order, dp_index, src, places):
    rows = src.shape[0] // len(order)
    per = len(order) // len(places)
    for at, rel in enumerate(order):
        place = pl.multiple_of((dp_index ^ rel) * rows, rows)
        ref, index = places[at // per]
        row = at % per * rows
        ref[(*index, slice(row, row + rows), slice(None))] = src[pl.ds(place, rows), :]


def ffn_kernel(
    nt, order, up_plan, down_plan, counts, seq_rows, scal_ref, nl_ref, vec_ref, bias_ref, cot_hbm, *rest
):
    up_pieces, down_pieces, rest = rest[: counts[0]], rest[counts[0] : sum(counts)], rest[sum(counts) :]
    count = len(rest) - 15
    dg_ref, sent_refs, kept_refs = rest[0], rest[1 : 1 + count // 2], rest[1 + count // 2 : 1 + count]
    sum_ref, result_hbm, gf_hbm = rest[1 + count : 4 + count]
    up, down, hidden, acc, cot, result, gf, product, up_sems, down_sems, more = rest[4 + count :]
    step = pl.program_id(0)
    rows = nl_ref.shape[0]
    width = up.shape[2]
    chunk = rows // 2
    load_cot = pltpu.make_async_copy(cot_hbm, cot, more.at[0])
    store_result = pltpu.make_async_copy(result, result_hbm, more.at[1])
    store_gf = pltpu.make_async_copy(gf, gf_hbm, more.at[2])
    groups = [(up_plan, up_pieces, up, up_sems), (down_plan, down_pieces, down, down_sems)]
    fetch_weights(scal_ref[0], groups, nt, [load_cot])

    @pl.when(step < nt)
    def _():
        r = jnp.minimum(step, nt - 1)
        bias = bias_ref[r]
        for m in range(rows // chunk):
            at = slice(m * chunk, (m + 1) * chunk)
            low = nl_ref[at, :]
            for n in range(width // 256):
                span = slice(n * 256, (n + 1) * 256)
                pre = mm(low, up[r, :, span]) + bias[:, span]
                cumulative, slope = normal_parts(pre)
                hidden[r, at, span] = (pre * cumulative).astype(BF16)
                dg_ref[0, at, span] = slope.astype(BF16)
            product_f32 = mm(hidden[r, at, :], down[r], 1, 1)
            acc[at, :] = jnp.where(step == 0, 0.0, acc[at, :]) + product_f32

    @pl.when(step == nt - 1)
    def _():
        load_cot.wait()
        sum_ref[...] = jnp.zeros_like(sum_ref)
        tail = 128

        def norm_step(m, carry):
            at = pl.ds(pl.multiple_of(m * tail, tail), tail)
            normed, rstd = norm_stats(nl_ref[at, :].astype(F32) + acc[at, :] + vec_ref[2:3, :])
            result[at, :] = (normed * vec_ref[3:4, :] + vec_ref[4:5, :]).astype(BF16)
            seq = lax.div(m * tail, seq_rows)
            place = scal_ref[1] + m * tail - seq * seq_rows
            place = place + lax.broadcasted_iota(jnp.int32, (tail, normed.shape[1]), 0)
            grad_out = jnp.where(place < scal_ref[3 + seq], cot[at, :].astype(F32), 0.0)
            grad = norm_back(normed, rstd, vec_ref[3:4, :], grad_out)
            low = grad.astype(BF16)
            gf[at, :] = low
            sum_ref[0:1, :] += jnp.sum(grad_out * normed, axis=0, keepdims=True)
            sum_ref[1:2, :] += jnp.sum(grad_out, axis=0, keepdims=True)
            sum_ref[2:3, :] += jnp.sum(low.astype(F32), axis=0, keepdims=True)
            return carry

        lax.fori_loop(0, rows // tail, norm_step, 0)
        store_result.start()
        store_gf.start()

    def gradient(refs):
        at = step - nt
        r = jnp.where(at < nt // 2, 2 * at + 1, 2 * at - nt)
        product[...] = mm(gf[...], hidden[r], 0, 0).astype(BF16)
        lay_rows(order, scal_ref[0], product, [(ref, (0,)) for ref in refs])

    @pl.when((step >= nt) & (step < nt + nt // 2))
    def _():
        gradient(sent_refs)

    @pl.when(step >= nt + nt // 2)
    def _():
        gradient(kept_refs)

    @pl.when(step == 2 * nt - 1)
    def _():
        store_result.wait()
        store_gf.wait()


def ffn_back_kernel(
    nt, order, up_plan, down_plan, counts, scal_ref, gf_ref, nl_ref, vec_ref, dg_ref, n1_hbm, r1_hbm, *rest
):
    up_pieces, down_pieces, rest = rest[: counts[0]], rest[counts[0] : sum(counts)], rest[sum(counts) :]
    count = len(rest) - 13
    sent_refs, kept_refs = rest[: count // 2], rest[count // 2 : count]
    bup_ref, gb_ref, sum_ref = rest[count : count + 3]
    up, down, acc, gp, product, n1, r1, up_sems, down_sems, more = rest[count + 3 :]
    r = pl.program_id(0)
    rows = gf_ref.shape[0]
    width = up.shape[2]
    chunk = rows // 2
    load_n1 = pltpu.make_async_copy(n1_hbm, n1, more.at[0])
    load_r1 = pltpu.make_async_copy(r1_hbm, r1, more.at[1])
    groups = [(down_plan, down_pieces, down, down_sems), (up_plan, up_pieces, up, up_sems)]
    fetch_weights(scal_ref[0], groups, nt, [load_n1, load_r1])
    bup_ref[...] = jnp.zeros_like(bup_ref)
    for m in range(rows // chunk):
        at = slice(m * chunk, (m + 1) * chunk)
        low = gf_ref[at, :]
        for n in range(width // 256):
            span = slice(n * 256, (n + 1) * 256)
            grad = mm(low, down[r, :, span]) * dg_ref[0, at, span].astype(F32)
            grad = grad.astype(BF16)
            gp[at, span] = grad
            bup_ref[0, 0:1, span] += jnp.sum(grad.astype(F32), axis=0, keepdims=True)
        acc[at, :] = jnp.where(r == 0, 0.0, acc[at, :]) + mm(gp[at, :], up[r], 1, 1)
    product[...] = mm(nl_ref[...], gp[...], 0, 0).astype(BF16)

    def places(refs):
        out = []
        for ref in refs:
            out += [(ref, (0,))] if len(ref.shape) == 3 else [(ref, (i, 0)) for i in range(ref.shape[0])]
        return out

    @pl.when(lax.rem(r, 2) == 1)
    def _():
        lay_rows(order, scal_ref[0], product, places(sent_refs))

    @pl.when(lax.rem(r, 2) == 0)
    def _():
        lay_rows(order, scal_ref[0], product, places(kept_refs))

    @pl.when(r == nt - 1)
    def _():
        load_n1.wait()
        load_r1.wait()
        sum_ref[...] = jnp.zeros_like(sum_ref)
        tail = 128

        def norm_step(m, carry):
            at = pl.ds(pl.multiple_of(m * tail, tail), tail)
            grad_first = gf_ref[at, :].astype(F32) + acc[at, :]
            normed = n1[at, :].astype(F32)
            low = norm_back(normed, r1[at, 0:1], vec_ref[0:1, :], grad_first).astype(BF16)
            gb_ref[at, :] = low
            sum_ref[0:1, :] += jnp.sum(grad_first * normed, axis=0, keepdims=True)
            sum_ref[1:2, :] += jnp.sum(grad_first, axis=0, keepdims=True)
            sum_ref[2:3, :] += jnp.sum(low.astype(F32), axis=0, keepdims=True)
            return carry

        lax.fori_loop(0, rows // tail, norm_step, 0)


def attend_back_kernel(
    nt,
    part,
    plan,
    count,
    scal_ref,
    gb_ref,
    p_ref,
    q_ref,
    kp_ref,
    vp_ref,
    ks_ref,
    bias_ref,
    px0_ref,
    px1_ref,
    x_hbm,
    heads_hbm,
    *rest,
):
    pieces, rest = rest[:count], rest[count:]
    if part == 0:
        dqx_more, back_more, dqx_ref, back_sent_ref, back_kept_ref, sum_ref, sent_hbm, kept_hbm = rest[:8]
    else:
        dqx_ref, back_ref, sum_ref, sent_hbm, kept_hbm = rest[:5]
    w, kst, vst, dq, dk, dv, x, heads, grads, sems, more = rest[-11:]
    step = pl.program_id(0)
    seq = scal_ref[2] ^ 1 ^ step
    pairs, kp2, pair_cols = kst.shape
    kp = kp2 // 2
    held = pairs * pair_cols
    half = nt // 2
    cols = held // half
    load_x = pltpu.make_async_copy(x_hbm, x, more.at[0])
    load_heads = pltpu.make_async_copy(
        heads_hbm.at[:, :, pl.ds(part * held, held)], heads, more.at[1]
    )

    def fetch():
        return piece_copies(plan, scal_ref[0] & 1, pieces, w, sems)

    @pl.when(step == 0)
    def _():
        for copy in fetch():
            copy.start()
        load_x.start()
        load_heads.start()
        sum_ref[...] = jnp.zeros_like(sum_ref)

    split_pairs(kp_ref, kst)
    split_pairs(vp_ref, vst)

    @pl.when(step == 0)
    def _():
        for copy in fetch():
            copy.wait()

    gb = gb_ref[seq]
    grad_heads = mm(gb, w[3], 1, 1).astype(BF16)
    lane = lax.broadcasted_iota(jnp.int32, (kp, pair_cols), 1) < pair_cols // 2
    for pair in range(pairs):
        span = slice(pair * pair_cols, (pair + 1) * pair_cols)
        probs = p_ref[0, :, pair * kp2 : (pair + 1) * kp2]
        grad = grad_heads[:, span]
        grad_probs = mm(grad, vst[pair], 1, 1)
        both = mm(probs, grad, 0, 0)
        dv[step, :, span] = jnp.where(lane, both[:kp], both[kp:]).astype(BF16)
        weighted = probs.astype(F32) * grad_probs
        parts = []
        for side in range(2):
            cut = slice(side * kp, (side + 1) * kp)
            total = jnp.sum(weighted[:, cut], axis=-1, keepdims=True)
            parts.append((weighted[:, cut] - probs[:, cut].astype(F32) * total).astype(BF16))
        grad_scores = jnp.concatenate(parts, 1)
        dq[seq, :, span] = (mm(grad_scores, kst[pair]) * SCALE).astype(BF16)
        both = mm(grad_scores, q_ref[0, :, span], 0, 0)
        dk[step, :, span] = jnp.where(lane, both[:kp], both[kp:]).astype(BF16)
    dqx = mm(dq[seq], w[0])
    ks = ks_ref[0][:, 0:1]
    sum_ref[0:1, :] += jnp.sum(dq[seq].astype(F32), axis=0, keepdims=True)
    sum_ref[1:2, :] += jnp.sum(dk[step].astype(F32) * ks, axis=0, keepdims=True)
    sum_ref[2:3, :] += jnp.sum(dv[step].astype(F32) * ks, axis=0, keepdims=True)
    back = mm(dk[step], w[1]) + mm(dv[step], w[2])
    low = bias_ref[:, part * held : (part + 1) * held].astype(BF16)
    terms = mm(low, dk[step], 1, 1)[1:2] + mm(low, dv[step], 1, 1)[2:3]
    terms = jnp.concatenate([jnp.broadcast_to(terms, (16, kp)), jnp.zeros((16, back.shape[1] - kp), F32)], 1)
    if part == 0:
        dqx_ref[0] = (gb.astype(F32) + dqx_more[0].astype(F32) + dqx).astype(BF16)

        def put(ref):
            ref[:kp] = (back + back_more[0, :kp].astype(F32)).astype(BF16)
            ref[kp:] = (terms + back_more[0, kp:].astype(F32)).astype(BF16)

        @pl.when(step == 0)
        def _():
            put(back_sent_ref)

        @pl.when(step == 1)
        def _():
            put(back_kept_ref)

    else:
        dqx_ref[0] = dqx.astype(BF16)
        back_ref[0, :kp] = back.astype(BF16)
        back_ref[0, kp:] = terms.astype(BF16)

    @pl.when(step == 1)
    def _():
        def stores(i):
            out = []
            for j in range(half):
                hbm = (sent_hbm if j % 2 else kept_hbm).at[(scal_ref[scal_ref.shape[0] - 1]) ^ i]
                out.append(
                    pltpu.make_async_copy(grads.at[i, pl.ds(j * cols, cols)], hbm, more.at[2 + i * half + j])
                )
            return out

        def flat(ref):
            return ref[...].reshape(ref.shape[0] * ref.shape[1], ref.shape[2])

        px = jnp.concatenate([px1_ref[...], px0_ref[...]], 0)
        load_x.wait()
        load_heads.wait()
        for i, (a, b) in enumerate(((dq, flat(x)), (dk, px), (dv, px), (heads, flat(gb_ref)))):
            grads[i] = mm(flat(a), b, 0, 0).astype(BF16)
            for copy in stores(i):
                copy.start()
        for i in range(4):
            for copy in stores(i):
                copy.wait()


def finish_kernel(scal_ref, x_ref, here_ref, back_kept_ref, back_other_ref, dqx_ref, sums0_ref, sums0_more, sums1_ref, sums2_ref, bup_ref, gi_ref, *rest):
    pack_refs, pack, total = rest[:4], rest[4], rest[5]
    step = pl.program_id(0)
    seq = scal_ref[2] ^ step
    rows, kp = here_ref.shape
    place = scal_ref[1] + lax.broadcasted_iota(jnp.int32, (rows, kp), 0)
    live = place < scal_ref[3 + seq]
    here = here_ref[...]
    masked = jnp.where(live, here, jnp.zeros_like(here))
    back = jnp.where(step == 0, back_kept_ref[...], back_other_ref[...])
    gi_ref[0] = (dqx_ref[0].astype(F32) + mm(masked, back[:kp])).astype(BF16)
    terms = mm(x_ref[0], back[:kp], 1, 1) + back[kp : kp + 1, :kp].astype(F32)
    terms = jnp.where(live, terms, 0.0)

    @pl.when(step == 0)
    def _():
        total[...] = terms

    @pl.when(step == 1)
    def _():
        both = total[...] + terms
        small = 16
        height = pack.shape[0] - small
        width = pack.shape[1]
        groups = width // kp
        for g in range(groups):
            span = slice(g * kp, (g + 1) * kp)
            count = min(height, rows - g * height)
            pack[:count, span] = both[g * height : g * height + count]
            if count < height:
                pack[count:height, span] = jnp.zeros((height - count, kp), F32)
        pieces = [sums1_ref[2:3], sums1_ref[0:2], sums2_ref[2:3], sums2_ref[0:2]]
        pieces.append(jnp.concatenate([sums0_ref[0:3], sums0_more[0:3]], 1))
        pieces += [bup_ref[j, 0:1] for j in range(bup_ref.shape[0])]
        count = sum(p.shape[0] for p in pieces)
        pieces.append(jnp.zeros((small - count, width), F32))
        pack[height:] = jnp.concatenate(pieces, 0)
        part = pack_refs[0].shape[0]
        for e, ref in enumerate(pack_refs):
            place = pl.multiple_of((scal_ref[scal_ref.shape[0] - 1] ^ e) * part, part)
            ref[...] = pack[pl.ds(place, part), :].astype(BF16)


def unpack_kernel(nt, small, scal_ref, *refs):
    parts, (out_ref, small_ref, held) = refs[:-3], refs[-3:]
    rows, kp = out_ref.shape[0] // nt, out_ref.shape[1]
    part = parts[0].shape[1]
    height = held.shape[1] - small
    for e, ref in enumerate(parts):
        place = pl.multiple_of((scal_ref[scal_ref.shape[0] - 1] ^ e) * part, part)
        held[:, pl.ds(place, part), :] = ref[...].astype(F32)
    for t in range(nt):
        base = (lax.div(scal_ref[1], rows) ^ t) * rows
        for g in range(held.shape[2] // kp):
            count = min(height, rows - g * height)
            place = pl.multiple_of(base + g * height, 16)
            out_ref[pl.ds(place, count), :] = held[t, :count, g * kp : (g + 1) * kp]
    small_ref[...] = held[:, height:, :]


def settle_kernel(scal_ref, *refs):
    parts, (qkv_ref, out_ref, held) = refs[:-3], refs[-3:]
    for e, ref in enumerate(parts):
        held[scal_ref[scal_ref.shape[0] - 1] ^ e] = ref[...].astype(F32)
    qkv_ref[...] = held[:3]
    out_ref[...] = held[3]


def whole(shape, buffers=None):
    mode = {} if buffers is None else {"pipeline_mode": pl.Buffered(buffers)}
    return pl.BlockSpec(shape, lambda *ids: (0,) * len(shape), **mode)


def call(kernel, name, grid, in_specs, out_specs, out_shapes, scratch, flops, moved, args):
    return pl.pallas_call(
        kernel,
        grid_spec=pltpu.PrefetchScalarGridSpec(
            num_scalar_prefetch=1, grid=grid, in_specs=in_specs, out_specs=out_specs, scratch_shapes=scratch
        ),
        out_shape=[jax.ShapeDtypeStruct(*s) for s in out_shapes],
        compiler_params=pltpu.CompilerParams(vmem_limit_bytes=VMEM_BYTES),
        cost_estimate=pl.CostEstimate(flops=flops, bytes_accessed=moved, transcendentals=0),
        name=name,
    )(*args)


ANY = pl.BlockSpec(memory_space=pl.ANY)


def project(scalars, x, length_proj):
    seqs, rows, width = x.shape
    kp = length_proj.shape[1]
    return call(
        functools.partial(project_kernel, seqs),
        "project",
        (seqs,),
        [
            pl.BlockSpec((1, rows, width), lambda i, s: (s[2] ^ 1 ^ i, 0, 0)),
            pl.BlockSpec((rows, kp), lambda i, s: (lax.div(s[1], rows), 0)),
            whole(length_proj.shape),
        ],
        [
            whole((kp, width)),
            whole((kp, width)),
            pl.BlockSpec((1, kp, 128), lambda i, s: (s[2] ^ 1 ^ i, 0, 0)),
        ],
        [((kp, width), BF16), ((kp, width), F32), ((seqs, kp, 128), F32)],
        [],
        1_000_000_000,
        5_000_000,
        (scalars, x, length_proj, length_proj),
    )


def attend(scalars, x, px0, px1, key_sum, plan, pieces, biases, vectors):
    seqs, rows, width = x.shape
    kp = px0.shape[0]
    pairs = width // (2 * DH)
    by_seq = lambda i, s: (s[2] ^ i, 0, 0)
    outs = [
        (rows, width, BF16),
        (rows, 2 * pairs * kp, BF16),
        (kp, width, BF16),
        (kp, width, BF16),
        (rows, width, BF16),
        (rows, width, BF16),
        (rows, width, BF16),
        (rows, 128, F32),
    ]
    return call(
        functools.partial(attend_kernel, plan, len(pieces)),
        "attend",
        (seqs,),
        [
            pl.BlockSpec((1, rows, width), by_seq),
            whole(px0.shape),
            whole(px1.shape),
            pl.BlockSpec((1, kp, 128), by_seq),
        ]
        + [ANY] * len(pieces)
        + [whole(biases.shape), whole(vectors.shape)],
        [pl.BlockSpec((1, r, c), by_seq) for r, c, _ in outs],
        [((seqs, r, c), t) for r, c, t in outs],
        [
            pltpu.VMEM((4, width, width), BF16),
            pltpu.VMEM((pairs, 2 * kp, 2 * DH), BF16),
            pltpu.VMEM((pairs, 2 * kp, 2 * DH), BF16),
            pltpu.SemaphoreType.DMA((len(plan),)),
        ],
        14_000_000_000,
        25_000_000,
        (scalars, x, px0, px1, key_sum, *pieces, biases, vectors),
    )


def ffn(order, parts, scalars, nl, vectors, biases, cotangent, up, down, seq_rows):
    rows, width = nl.shape
    nt, _, hidden = biases.shape
    half = nt // 2
    (up_plan, up_pieces), (down_plan, down_pieces) = up, down
    counts = (len(up_pieces), len(down_pieces))
    rows_in = width
    part = width // parts
    return call(
        functools.partial(ffn_kernel, nt, order, up_plan, down_plan, counts, seq_rows),
        "feed_forward",
        (2 * nt,),
        [whole((rows, width), 1), whole(vectors.shape), whole(biases.shape), ANY] + [ANY] * sum(counts),
        [
            pl.BlockSpec((1, rows, hidden), lambda i, s: (jnp.minimum(i, nt - 1), 0, 0)),
            *[pl.BlockSpec((1, part, hidden), lambda i, s: (jnp.clip(i - nt, 0, half - 1), 0, 0))] * parts,
            *[pl.BlockSpec((1, part, hidden), lambda i, s: (jnp.clip(i - nt - half, 0, half - 1), 0, 0))] * parts,
            whole((8, width)),
            ANY,
            ANY,
        ],
        [
            ((nt, rows, hidden), BF16),
            *[((half, part, hidden), BF16)] * (2 * parts),
            ((8, width), F32),
            ((rows, width), BF16),
            ((rows, width), BF16),
        ],
        [
            pltpu.VMEM((nt, rows_in, hidden), BF16),
            pltpu.VMEM((nt, rows_in, hidden), BF16),
            pltpu.VMEM((nt, rows, hidden), BF16),
            pltpu.VMEM((rows, width), F32),
            pltpu.VMEM((rows, width), BF16),
            pltpu.VMEM((rows, width), BF16),
            pltpu.VMEM((rows, width), BF16),
            pltpu.VMEM((rows_in, hidden), BF16),
            pltpu.SemaphoreType.DMA((len(up_plan),)),
            pltpu.SemaphoreType.DMA((len(down_plan),)),
            pltpu.SemaphoreType.DMA((3,)),
        ],
        24_000_000_000,
        30_000_000,
        (scalars, nl, vectors, biases, cotangent, *up_pieces, *down_pieces),
    )


def ffn_back(order, parts, scalars, gf, nl, vectors, slopes, n1, r1, up, down):
    rows, width = n1.shape
    nt, _, hidden = slopes.shape
    half = nt // 2
    part = width // parts
    (up_plan, up_pieces), (down_plan, down_pieces) = up, down
    counts = (len(up_pieces), len(down_pieces))
    by_chip = [pl.BlockSpec((1, part, hidden), lambda i, s: (lax.div(i, 2), 0, 0))]
    chip_shapes = [((half, part, hidden), BF16)]
    if parts > 1:
        by_chip.append(pl.BlockSpec((parts - 1, 1, part, hidden), lambda i, s: (0, lax.div(i, 2), 0, 0)))
        chip_shapes.append(((parts - 1, half, part, hidden), BF16))
    return call(
        functools.partial(ffn_back_kernel, nt, order, up_plan, down_plan, counts),
        "feed_forward_back",
        (nt,),
        [
            whole((rows, width), 1),
            whole((rows, width), 1),
            whole(vectors.shape),
            pl.BlockSpec((1, rows, hidden), lambda i, s: (i, 0, 0)),
            ANY,
            ANY,
        ]
        + [ANY] * sum(counts),
        [
            *by_chip,
            *by_chip,
            pl.BlockSpec((1, 8, hidden), lambda i, s: (i, 0, 0)),
            whole((rows, width)),
            whole((8, width)),
        ],
        [
            *chip_shapes,
            *chip_shapes,
            ((nt, 8, hidden), F32),
            ((rows, width), BF16),
            ((8, width), F32),
        ],
        [
            pltpu.VMEM((nt, width, hidden), BF16),
            pltpu.VMEM((nt, width, hidden), BF16),
            pltpu.VMEM((rows, width), F32),
            pltpu.VMEM((rows, hidden), BF16),
            pltpu.VMEM((width, hidden), BF16),
            pltpu.VMEM((rows, width), BF16),
            pltpu.VMEM((rows, 128), F32),
            pltpu.SemaphoreType.DMA((len(up_plan),)),
            pltpu.SemaphoreType.DMA((len(down_plan),)),
            pltpu.SemaphoreType.DMA((2,)),
        ],
        24_000_000_000,
        25_000_000,
        (scalars, gf, nl, vectors, slopes, n1, r1, *up_pieces, *down_pieces),
    )


def attend_back(nt, part, scalars, gb, probs, q, kproj, vproj, key_sum, biases, px0, px1, x, heads, plan, pieces, more):
    seqs, rows, width = gb.shape
    kp = kproj.shape[1]
    half = nt // 2
    cols = width // nt
    pairs = width // (4 * DH)
    held = width // 2
    plan = [(p, row, block - 2 * part, kind, turned) for p, row, block, kind, turned in plan if block // 2 == part]
    by_seq = lambda i, s: (s[2] ^ 1 ^ i, 0, 0)
    by_part = lambda i, s: (s[2] ^ 1 ^ i, 0, part)
    rows_block = pl.BlockSpec((1, rows, width), by_seq)
    back_block = pl.BlockSpec((1, kp + 16, width), by_seq)
    back_specs = [back_block] if part else [whole((kp + 16, width)), whole((kp + 16, width))]
    back_shapes = [((seqs, kp + 16, width), BF16)] if part else [((kp + 16, width), BF16)] * 2
    return call(
        functools.partial(attend_back_kernel, nt, part, plan, len(pieces)),
        "attend_back",
        (seqs,),
        [
            whole(gb.shape, 1),
            pl.BlockSpec((1, rows, 2 * pairs * kp), by_part),
            pl.BlockSpec((1, rows, held), by_part),
            pl.BlockSpec((1, kp, held), by_part),
            pl.BlockSpec((1, kp, held), by_part),
            pl.BlockSpec((1, kp, 128), by_seq),
            whole(biases.shape),
            whole(px0.shape),
            whole(px1.shape),
            ANY,
            ANY,
        ]
        + [ANY] * len(pieces)
        + ([] if part else [rows_block, back_block]),
        [rows_block, *back_specs, whole((8, held)), ANY, ANY],
        [
            ((seqs, rows, width), BF16),
            *back_shapes,
            ((8, held), F32),
            ((4, cols, width), BF16),
            ((4, cols, width), BF16),
        ],
        [
            pltpu.VMEM((4, held, width), BF16),
            pltpu.VMEM((pairs, 2 * kp, 2 * DH), BF16),
            pltpu.VMEM((pairs, 2 * kp, 2 * DH), BF16),
            pltpu.VMEM((seqs, rows, held), BF16),
            pltpu.VMEM((seqs, kp, held), BF16),
            pltpu.VMEM((seqs, kp, held), BF16),
            pltpu.VMEM((seqs, rows, width), BF16),
            pltpu.VMEM((seqs, rows, held), BF16),
            pltpu.VMEM((4, held, width), BF16),
            pltpu.SemaphoreType.DMA((len(plan),)),
            pltpu.SemaphoreType.DMA((2 + 4 * half,)),
        ],
        10_000_000_000,
        18_000_000,
        (scalars, gb, probs, q, kproj, vproj, key_sum, biases, px0, px1, x, heads, *pieces, *more),
    )


def finish(scalars, x, length_proj, back_kept, back_other, dqx, sums0, sums0_more, sums1, sums2, bup, pack_rows):
    seqs, rows, width = x.shape
    kp = length_proj.shape[1]
    by_seq = lambda i, s: (s[2] ^ i, 0, 0)
    return call(
        finish_kernel,
        "finish",
        (seqs,),
        [
            pl.BlockSpec((1, rows, width), by_seq),
            pl.BlockSpec((rows, kp), lambda i, s: (lax.div(s[1], rows), 0)),
            whole(back_kept.shape),
            whole(back_other.shape),
            pl.BlockSpec((1, rows, width), by_seq),
            whole(sums0.shape),
            whole(sums0_more.shape),
            whole(sums1.shape),
            whole(sums2.shape),
            whole(bup.shape),
        ],
        [pl.BlockSpec((1, rows, width), by_seq), *[whole((pack_rows // 4, width))] * 4],
        [((seqs, rows, width), BF16), *[((pack_rows // 4, width), BF16)] * 4],
        [pltpu.VMEM((pack_rows, width), F32), pltpu.VMEM((rows, kp), F32)],
        2_000_000_000,
        6_000_000,
        (scalars, x, length_proj, back_kept, back_other, dqx, sums0, sums0_more, sums1, sums2, bup),
    )


def unpack(scalars, parts, rows, kp, small):
    nt, part, width = parts[0].shape
    height = 4 * part
    return call(
        functools.partial(unpack_kernel, nt, small),
        "unpack",
        (),
        [whole(p.shape) for p in parts],
        [whole((nt * rows, kp)), whole((nt, small, width))],
        [((nt * rows, kp), F32), ((nt, small, width), F32)],
        [pltpu.VMEM((nt, height, width), F32)],
        1_000_000,
        4_000_000,
        (scalars, *parts),
    )


def settle(scalars, parts):
    rows, width = parts[0].shape
    return call(
        settle_kernel,
        "settle",
        (),
        [whole(p.shape) for p in parts],
        [whole((3, rows, width)), whole((rows, width))],
        [((3, rows, width), F32), ((rows, width), F32)],
        [pltpu.VMEM((4, rows, width), F32)],
        1_000_000,
        4_000_000,
        (scalars, *parts),
    )


def local(
    dp,
    tp,
    inputs,
    lengths,
    w_qkv,
    b_qkv,
    output_weight,
    b_out,
    length_proj,
    first_gain,
    first_shift,
    w_up,
    hidden_bias,
    w_down,
    b_down,
    second_gain,
    second_shift,
    cotangent,
):
    seqs, local_len, width = inputs.shape
    cols = w_qkv.shape[2]
    kp = length_proj.shape[1]
    hidden_cols = w_up.shape[1]
    block_rows = w_up.shape[0]
    tbits, dbits = bits_of(tp), bits_of(dp)
    t_index = lax.axis_index("tensor")
    rows_count = seqs * local_len
    relative = block_rows % 16 == 0 and (tp, dp) == (4, 8)

    dp_index = lax.axis_index("dp")
    if relative:
        y, z, zz = dbits
        square_xy = [0, zz, z, z ^ zz]
        square_xy = square_xy + [o ^ y for o in square_xy]
        square_yz = [o ^ zz * half for o in (y ^ z, 0, y, z) for half in range(2)]
    else:
        square_xy = square_yz = [0]
        dp_index = jnp.zeros((), jnp.int32)
    where = jnp.stack([dp_index, t_index * local_len, t_index & 1]).astype(jnp.int32)
    quarter = (lax.axis_index("dp") & 3).astype(jnp.int32)
    scalars = jnp.concatenate([where, lengths.astype(jnp.int32), quarter[None]])
    vectors = jnp.stack(
        [first_gain, first_shift, b_down, second_gain, second_shift, b_out, b_out, b_out]
    )

    core, chip = tbits

    def over_core(value):
        return swap(value, "tensor", core, tp)

    def over_chip(value):
        return swap(value, "tensor", chip, tp)

    def over_dp(value, bit):
        return swap(value, "dp", bit, dp)

    line = Line()

    def gather_tensor(value):
        both = [value, over_chip(value)]
        return [v for b in both for v in (b, over_core(b))]

    qkv_rows = w_qkv.transpose(1, 2, 0)
    halves = jnp.where(own_bit("dp", 1), jnp.stack([qkv_rows[2], output_weight]), qkv_rows[:2])
    first = over_chip(halves.reshape(2 * cols, width))
    bias_rows = jnp.zeros((8, width), F32)
    bias_rows = bias_rows.at[0:3, :cols].set(b_qkv).at[3, :hidden_cols].set(hidden_bias)
    bias_all = jnp.stack(gather_tensor(bias_rows))
    biases = jnp.pad(bias_all[:, :3, :cols].transpose(1, 0, 2).reshape(3, tp * cols), ((0, 5), (0, 0)))
    bias_hidden = bias_all[:, 3:4, :hidden_cols]

    def plan_of(pieces, blocks):
        rows = sum(p.shape[0] for p in pieces) // sum(len(b) for b in blocks)
        plan = [(i, k * rows, r, rel) for i, b in enumerate(blocks) for k, (r, rel) in enumerate(b)]
        plan += [(i + len(pieces), row, r + 1, rel) for i, row, r, rel in plan]
        return plan, pieces + [over_core(p) for p in pieces]

    if relative:
        a_far, m_far = over_dp(w_up, zz), over_dp(w_down, zz)

    sent, kept, key_sum = project(scalars, inputs, length_proj)
    if relative:
        sent, kept, a_far = line.meet(sent, kept, a_far)
        a = jnp.concatenate([w_up, a_far], 0)
        a_near = over_dp(a, z)
        px0, m_far, first = line.meet(over_core(sent), m_far, first)
        m = jnp.concatenate([w_down, m_far], 0)
        m_chip = over_chip(m)
    else:
        px0, first = line.meet(over_core(sent), first)
    px0 = add(kept, px0)
    px_chip = over_chip(px0)
    second = over_dp(first, 1)
    if relative:
        a_near = line.meet(a_near)
        a = jnp.concatenate([a, a_near], 0)
        b = over_dp(a, y)
        m_chip, px_chip = line.meet(m_chip, px_chip)
        m = jnp.concatenate([m, m_chip], 0)
        my, mz, a1 = over_dp(m, y), over_dp(m, z), over_chip(a)
    else:
        px_chip = line.meet(px_chip)
    px0 = add(px0, px_chip)
    px1 = over_core(px0)
    if relative:
        second, b = line.meet(second, b)
        b1 = over_chip(b)
    else:
        second = line.meet(second)
    pieces = [qkv_rows.reshape(3 * cols, width), output_weight, first, second]
    pieces = pieces + [over_core(p) for p in pieces]
    plan = [(0, i * cols, 0, i, False) for i in range(3)] + [(1, 0, 0, 3, False)]
    plan += [(2, i * cols, 2, i, True) for i in range(2)] + [(3, i * cols, 2, i ^ 2, True) for i in range(2)]
    plan += [(p + 4, row, block + 1, kind, turned) for p, row, block, kind, turned in plan]
    if relative:
        my, mz = line.meet(my, mz)
        myz = over_dp(my, z)

    q, probs, kproj, vproj, heads, n1, nl, r1 = attend(
        scalars, line.after(inputs), px0, px1, key_sum, plan, pieces, biases, vectors
    )
    nl, n1, r1 = (v.reshape(rows_count, -1) for v in (nl, n1, r1))
    if relative:
        nl, a1, b1, myz = line.meet(nl, a1, b1, myz)
        orders = [square_xy[:4], square_xy[4:]]
        up = plan_of([a, b, a1, b1], [[(r, o) for o in half] for r in (0, 2) for half in orders])
        blocks = [[(r, o ^ e) for r in (0, 2) for e in (0, zz)] for o in (0, y, z, y ^ z)]
        down = plan_of([m, my, mz, myz], blocks)
    else:
        nl = line.meet(nl)
        pieces_up, pieces_down = (lax.all_gather(w, "dp", axis=0, tiled=True) for w in (w_up, w_down))
        up = plan_of([pieces_up, over_chip(pieces_up)], [[(0, 0)], [(2, 0)]])
        down = plan_of([pieces_down, over_chip(pieces_down)], [[(0, 0)], [(2, 0)]])
    parts = 2 if relative else 1
    outs = ffn(
        square_xy,
        parts,
        scalars,
        nl,
        vectors,
        bias_hidden,
        cotangent.reshape(rows_count, width),
        up,
        down,
        local_len,
    )
    slopes, down_sent, down_kept = outs[0], outs[1 : 1 + parts], outs[1 + parts : 1 + 2 * parts]
    sums2, result, gf = outs[1 + 2 * parts :]

    def scatter_plain(kept, got):
        value = add(kept, got)
        value = add(value[0], over_chip(value[1])).astype(F32)
        return lax.psum_scatter(value, "dp", scatter_dimension=0, tiled=True)

    if relative:
        got_b, got_a = over_core(down_sent[1]), over_core(down_sent[0])
        gf, got_b = line.meet(gf, got_b)
        b1 = add(down_kept[1][1], got_b[1])
        got_b1 = over_dp(b1, y)
        gf, b1 = line.meet(gf, b1)
    else:
        got_down = over_core(down_sent[0])
        gf = line.meet(gf)
    outs = ffn_back(
        square_yz, 4 if relative else 1, scalars, line.after(gf), nl, vectors, slopes, n1, r1, up, down
    )
    bup, gb, sums1 = outs[-3:]
    if relative:
        up_sent, up_sent_more, up_kept, up_kept_more = outs[:4]
        gb, up_sent, got_a, got_b1 = line.meet(gb, up_sent, got_a, got_b1)
        a1 = add(down_kept[0][1], got_a[1], got_b1)
        b = add(down_kept[1][0], got_b[0])
        got_a1, got_b = over_chip(a1), over_dp(b, y)
        got_up, got_up_more = over_core(up_sent), over_core(up_sent_more)
        got_up = line.meet(got_up)
        myz = add(up_kept, got_up)
        got_myz = over_dp(myz, z)
        gb, myz = line.meet(gb, myz)
    else:
        up_sent, up_kept = outs[:2]
        got_up = over_core(up_sent)
        down_weight_gradient = scatter_plain(down_kept[0], got_down)
        up_weight_gradient = scatter_plain(up_kept, got_up)
        gb = line.meet(gb)

    def heads_back(part, more):
        return attend_back(
            tp,
            part,
            scalars,
            line.after(gb).reshape(seqs, local_len, width),
            probs,
            q,
            kproj,
            vproj,
            key_sum,
            biases,
            px0,
            px1,
            inputs,
            heads,
            plan,
            pieces,
            more,
        )

    dqx, back, sums0_more, sent1, kept1 = heads_back(1, [])
    if relative:
        sent1, kept1, got_a1, got_b, got_myz, got_up_more = line.meet(
            sent1, kept1, got_a1, got_b, got_myz, got_up_more
        )
        a = add(down_kept[0][0], got_a[0], got_a1, got_b)
        a, a_sent = a[: 2 * block_rows], a[2 * block_rows :]
        got_a = over_dp(a_sent, z)
        m, my, mz = (add(up_kept_more[i], got_up_more[i]) for i in range(3))
        my = add(my, got_myz)
        got_my, got_mz = over_dp(my, y), over_dp(mz, z)
    else:
        sent1, kept1 = line.meet(sent1, kept1)
    got1 = line.meet(over_core(sent1))
    attn1 = add(kept1, got1)
    got_attn = over_chip(attn1[:3])
    gb, attn1 = line.meet(gb, attn1)
    dqx, back_sent, back_kept, sums0, sent0, kept0 = heads_back(0, [dqx, back])

    if relative:
        back_sent, back_kept, sent0, kept0, got_attn, got_a, got_my, got_mz = line.meet(
            back_sent, back_kept, sent0, kept0, got_attn, got_a, got_my, got_mz
        )
    else:
        back_sent, back_kept, sent0, kept0, got_attn = line.meet(back_sent, back_kept, sent0, kept0, got_attn)
    got_back, got0, got_attn_last = over_core(back_sent), over_core(sent0), over_chip(attn1[3])
    if relative:
        a = add(a, got_a)
        got_a = over_dp(a[block_rows:], zz)
        m = add(m, got_my, got_mz)
        got_m = over_chip(m[1])
    back_kept = add(back_kept, line.meet(got_back))
    got_back = over_chip(back_kept)
    got0, got_attn_last = line.meet(got0, got_attn_last)

    near, further = dbits[:2], dbits[2:]
    corners = [0, near[0], near[1], near[0] ^ near[1]]
    attn = [add(kept0[e], got0[e], got_attn[e]) for e in range(3)] + [add(kept0[3], got0[3], got_attn_last)]
    got_attn = [over_dp(attn[e], corners[e]) for e in (1, 2, 3)]
    if relative:
        got_a, got_m = line.meet(got_a, got_m)
        down_weight_gradient = a[:block_rows].astype(F32) + got_a.astype(F32)
        m = add(m[0], got_m)
        got_m = over_dp(m[block_rows:], zz)
    back_kept = add(back_kept, line.meet(got_back))
    back_other = line.meet(over_core(back_kept))
    small = 16
    height = -(-local_len * kp // width // 16) * 16
    grad_inputs, *shared = finish(
        scalars,
        inputs,
        length_proj,
        back_kept,
        back_other,
        dqx,
        sums0,
        sums0_more,
        sums1,
        sums2,
        bup,
        height + small,
    )
    if relative:
        met = line.meet(*shared, got_m, *got_attn)
        shared, got_m, got_attn = met[:4], met[4], met[5:]
        up_weight_gradient = m[:block_rows].astype(F32) + got_m.astype(F32)
    else:
        met = line.meet(*shared, *got_attn)
        shared, got_attn = met[:4], met[4:]
    got_shared = [over_dp(shared[e], corners[e]) for e in (1, 2, 3)]
    attn = add_pairs(attn[0], *got_attn)

    def over_rest(value):
        for bit in further[1:]:
            value = add(value, over_dp(value, bit))
        return value

    got = over_dp(attn, further[0])
    got_shared = line.meet(*got_shared)
    shared = add_pairs(shared[0], *got_shared)
    got_more = over_dp(shared, further[0])
    got, got_more = line.meet(got, got_more)
    attn, shared = over_rest(add(attn, got)), over_rest(add(shared, got_more))
    got_attn = [over_dp(attn, corners[e]) for e in (1, 2, 3)]
    shared = jnp.stack([shared, line.meet(over_chip(shared))])
    shared = jnp.stack([shared, line.meet(over_core(shared))], 1).reshape(tp, -1, width)
    got_shared = [over_dp(shared, corners[e]) for e in (1, 2, 3)]
    got_attn = line.meet(*got_attn)
    grad_w_qkv, grad_w_out = settle(scalars, [attn, *got_attn])
    grad_w_qkv = grad_w_qkv.transpose(2, 0, 1)
    got_shared = line.meet(*got_shared)
    grad_length_proj, rows = unpack(scalars, [shared, *got_shared], local_len, kp, small)
    whole_sum = [jnp.sum(rows[:, i], axis=0) for i in range(6)]

    def own_block(picked):
        size = picked.shape[1] // tp
        return functools.reduce(jnp.add, [picked[r, r * size : (r + 1) * size] for r in range(tp)])

    grad_b_qkv = jnp.stack([own_block(rows[:, 6 + i]) for i in range(3)])
    grad_b_up = own_block(rows[:, 9 : 9 + tp].reshape(tp, tp * width)[:, : tp * hidden_cols])

    shape = (seqs, local_len, width)
    return (
        result.reshape(shape),
        grad_inputs,
        grad_w_qkv,
        grad_b_qkv,
        grad_w_out,
        whole_sum[0],
        grad_length_proj,
        whole_sum[1],
        whole_sum[2],
        up_weight_gradient,
        grad_b_up,
        down_weight_gradient,
        whole_sum[3],
        whole_sum[4],
        whole_sum[5],
    )


def solution(mesh):
    placed = (
        P("dp", "tensor", None),
        P("dp"),
        P(None, None, "tensor"),
        P(None, "tensor"),
        P("tensor", None),
        P(),
        P(),
        P(),
        P(),
        P("dp", "tensor"),
        P("tensor"),
        P("dp", "tensor"),
        P(),
        P(),
        P(),
        P("dp", "tensor", None),
    )
    return jax.shard_map(
        functools.partial(local, mesh.shape["dp"], mesh.shape["tensor"]),
        mesh=mesh,
        in_specs=placed,
        out_specs=(
            P("dp", "tensor", None),
            P("dp", "tensor", None),
            P(None, None, "tensor"),
            P(None, "tensor"),
            P("tensor", None),
            P(),
            P(),
            P(),
            P(),
            P("dp", "tensor"),
            P("tensor"),
            P("dp", "tensor"),
            P(),
            P(),
            P(),
        ),
        check_vma=False,
    )
```

```python
import functools

import jax
import jax.numpy as jnp
from jax import lax
from jax.experimental import pallas as pl
from jax.experimental.pallas import tpu as pltpu
from jax.sharding import PartitionSpec as P

DH = 64
SCALE = DH ** (-0.5)
EPS = 1e-05
F32 = jnp.float32
BF16 = jnp.bfloat16
VMEM_BYTES = 58 * 1024 * 1024


def bits_of(size):
    count = size.bit_length() - 1
    assert 1 << count == size
    return [1 << b for b in range(count)]


class Line:
    def __init__(self):
        self.last = None

    def meet(self, *values):
        count = len(values)
        values = lax.optimization_barrier(values if self.last is None else (*values, self.last))
        self.last = values[0]
        return values[0] if count == 1 else values[:count]

    def after(self, value):
        return lax.optimization_barrier((value, self.last))[0]


def swap(value, axis, bit, size):
    return lax.ppermute(value, axis, [(i, i ^ bit) for i in range(size)])


def own_bit(axis, bit):
    return (lax.axis_index(axis) & bit) != 0


def add(a, *more):
    for b in more:
        a = a.astype(F32) + b.astype(F32)
    return a.astype(BF16)


def add_pairs(a, b, c, d):
    a, b, c, d = (v.astype(F32) for v in (a, b, c, d))
    return ((a + b) + (c + d)).astype(BF16)


def norm_stats(rows):
    center = jnp.mean(rows, axis=-1, keepdims=True)
    offsets = rows - center
    rstd = lax.rsqrt(jnp.mean(offsets * offsets, axis=-1, keepdims=True) + EPS)
    return offsets * rstd, rstd


def norm_back(normed, rstd, gain, grad):
    g = grad * gain
    return rstd * (
        g
        - jnp.mean(g, axis=-1, keepdims=True)
        - normed * jnp.mean(g * normed, axis=-1, keepdims=True)
    )


def mm(a, b, ca=1, cb=0):
    return lax.dot_general(a, b, (((ca,), (cb,)), ((), ())), preferred_element_type=F32)


def normal_parts(values):
    cumulative = 0.5 + 0.5 * lax.erf(values * 0.7071067811865476)
    return cumulative, cumulative + values * jnp.exp(values * values * -0.5) * 0.3989422804014327


def project_kernel(seqs, scal_ref, x_ref, here_ref, all_ref, sent_ref, kept_ref, sum_ref):
    step = pl.program_id(0)
    seq = scal_ref[2] ^ 1 ^ step
    length = scal_ref[3 + seq]
    rows, kp = here_ref.shape
    place = scal_ref[1] + lax.broadcasted_iota(jnp.int32, (rows, kp), 0)
    here = here_ref[...]
    masked = jnp.where(place < length, here, jnp.zeros_like(here))
    part = mm(masked, x_ref[0], 0, 0)

    @pl.when(step == 0)
    def _():
        sent_ref[...] = part.astype(BF16)

    @pl.when(step == 1)
    def _():
        kept_ref[...] = part

    place = lax.broadcasted_iota(jnp.int32, all_ref.shape, 0)
    every = all_ref[...]
    masked = jnp.where(place < length, every, jnp.zeros_like(every))
    sum_ref[0] = mm(masked, jnp.ones((all_ref.shape[0], 128), BF16), 0, 0)


def split_pairs(src, dst):
    pairs, kp2, pair_cols = dst.shape
    kp = kp2 // 2
    lane = lax.broadcasted_iota(jnp.int32, (kp, pair_cols), 1) < pair_cols // 2
    for pair in range(pairs):
        both = src[0, :, pair * pair_cols : (pair + 1) * pair_cols]
        zero = jnp.zeros_like(both)
        dst[pair, :kp] = jnp.where(lane, both, zero)
        dst[pair, kp:] = jnp.where(lane, zero, both)


def piece_copies(plan, split, pieces, w, sems):
    cols = pieces[0].shape[1] // 4
    copies = []
    for at, (piece, row, block, kind, turned) in enumerate(plan):
        kind = kind ^ (2 * split) if turned else kind
        copies.append(
            pltpu.make_async_copy(
                pieces[piece].at[pl.ds(row, cols)], w.at[kind, pl.ds(block * cols, cols)], sems.at[at]
            )
        )
    return copies


def attend_kernel(plan, count, scal_ref, x_ref, px0_ref, px1_ref, ks_ref, *rest):
    pieces = rest[:count]
    bias_ref, vec_ref = rest[count : count + 2]
    q_ref, p_ref, kp_ref, vp_ref, heads_ref, n1_ref, nl_ref, r1_ref = rest[count + 2 : count + 10]
    w, kst, vst, sems = rest[count + 10 :]
    step = pl.program_id(0)
    pairs, kp2, pair_cols = kst.shape
    kp = kp2 // 2

    @pl.when(step == 0)
    def _():
        copies = piece_copies(plan, scal_ref[0] & 1, pieces, w, sems)
        for copy in copies:
            copy.start()
        for copy in copies:
            copy.wait()

    px = jnp.where(step == 0, px0_ref[...], px1_ref[...])
    ks = ks_ref[0][:, 0:1]
    kp_ref[0] = (mm(px, w[1], 1, 1) + ks * bias_ref[1:2, :]).astype(BF16)
    vp_ref[0] = (mm(px, w[2], 1, 1) + ks * bias_ref[2:3, :]).astype(BF16)
    split_pairs(kp_ref, kst)
    split_pairs(vp_ref, vst)

    x = x_ref[0]
    q_ref[0] = ((mm(x, w[0], 1, 1) + bias_ref[0:1, :]).astype(BF16) * SCALE).astype(BF16)
    for pair in range(pairs):
        span = slice(pair * pair_cols, (pair + 1) * pair_cols)
        scores = mm(kst[pair], q_ref[0, :, span], 1, 1)
        for side in range(2):
            part = scores[side * kp : (side + 1) * kp]
            raised = jnp.exp(part - jnp.max(part, axis=0, keepdims=True))
            part = raised * (1.0 / jnp.sum(raised, axis=0, keepdims=True))
            row = pair * kp2 + side * kp
            p_ref[0, row : row + kp, :] = part.astype(BF16)
        heads_ref[0, :, span] = mm(p_ref[0, pair * kp2 : (pair + 1) * kp2, :], vst[pair], 0, 0).astype(BF16)
    resid = x.astype(F32) + mm(heads_ref[0], w[3]) + vec_ref[5:6, :]
    normed, rstd = norm_stats(resid)
    n1_ref[0] = normed.astype(BF16)
    nl_ref[0] = (normed * vec_ref[0:1, :] + vec_ref[1:2, :]).astype(BF16)
    r1_ref[0] = jnp.broadcast_to(rstd, r1_ref.shape[1:])


def weight_copies(plan, dp_index, pieces, dst, sems, r):
    rows = sum(ref.shape[0] for ref in pieces) // len(plan)
    copies = []
    for at, (piece, row, block, rel) in enumerate(plan):
        if block == r:
            place = pl.multiple_of((dp_index ^ rel) * rows, rows)
            copies.append(
                pltpu.make_async_copy(
                    pieces[piece].at[pl.ds(row, rows)], dst.at[r, pl.ds(place, rows)], sems.at[at]
                )
            )
    return copies


def fetch_weights(dp_index, groups, nt, extra=()):
    step = pl.program_id(0)

    @pl.when(step == 0)
    def _():
        for r in range(nt):
            for plan, pieces, dst, sems in groups:
                for copy in weight_copies(plan, dp_index, pieces, dst, sems, r):
                    copy.start()
        for copy in extra:
            copy.start()

    for r in range(nt):

        @pl.when(step == r)
        def _():
            for plan, pieces, dst, sems in groups:
                for copy in weight_copies(plan, dp_index, pieces, dst, sems, r):
                    copy.wait()


def lay_rows(order, dp_index, src, places):
    rows = src.shape[0] // len(order)
    per = len(order) // len(places)
    for at, rel in enumerate(order):
        place = pl.multiple_of((dp_index ^ rel) * rows, rows)
        ref, index = places[at // per]
        row = at % per * rows
        ref[(*index, slice(row, row + rows), slice(None))] = src[pl.ds(place, rows), :]


def ffn_kernel(
    nt, order, up_plan, down_plan, counts, seq_rows, scal_ref, nl_ref, vec_ref, bias_ref, cot_hbm, *rest
):
    up_pieces, down_pieces, rest = rest[: counts[0]], rest[counts[0] : sum(counts)], rest[sum(counts) :]
    count = len(rest) - 15
    dg_ref, sent_refs, kept_refs = rest[0], rest[1 : 1 + count // 2], rest[1 + count // 2 : 1 + count]
    sum_ref, result_hbm, gf_hbm = rest[1 + count : 4 + count]
    up, down, hidden, acc, cot, result, gf, product, up_sems, down_sems, more = rest[4 + count :]
    step = pl.program_id(0)
    rows = nl_ref.shape[0]
    width = up.shape[2]
    chunk = rows // 4
    load_cot = pltpu.make_async_copy(cot_hbm, cot, more.at[0])
    store_result = pltpu.make_async_copy(result, result_hbm, more.at[1])
    store_gf = pltpu.make_async_copy(gf, gf_hbm, more.at[2])
    groups = [(up_plan, up_pieces, up, up_sems), (down_plan, down_pieces, down, down_sems)]
    fetch_weights(scal_ref[0], groups, nt, [load_cot])

    def rows_step(r, m):
        at = slice(m * chunk, (m + 1) * chunk)
        bias = bias_ref[r]
        low = nl_ref[at, :]
        for n in range(width // 256):
            span = slice(n * 256, (n + 1) * 256)
            pre = mm(low, up[r, :, span]) + bias[:, span]
            cumulative, slope = normal_parts(pre)
            hidden[r, at, span] = (pre * cumulative).astype(BF16)
            dg_ref[0, at, span] = slope.astype(BF16)
        return mm(hidden[r, at, :], down[r], 1, 1)

    def norm_step(at, first, branch):
        normed, rstd = norm_stats(nl_ref[at, :].astype(F32) + branch + vec_ref[2:3, :])
        result[at, :] = (normed * vec_ref[3:4, :] + vec_ref[4:5, :]).astype(BF16)
        seq = first // seq_rows
        place = scal_ref[1] + first - seq * seq_rows
        place = place + lax.broadcasted_iota(jnp.int32, normed.shape, 0)
        grad_out = jnp.where(place < scal_ref[3 + seq], cot[at, :].astype(F32), 0.0)
        low = norm_back(normed, rstd, vec_ref[3:4, :], grad_out).astype(BF16)
        gf[at, :] = low
        sum_ref[0:1, :] += jnp.sum(grad_out * normed, axis=0, keepdims=True)
        sum_ref[1:2, :] += jnp.sum(grad_out, axis=0, keepdims=True)
        sum_ref[2:3, :] += jnp.sum(low.astype(F32), axis=0, keepdims=True)

    @pl.when(step < nt - 1)
    def _():
        r = jnp.minimum(step, nt - 1)
        for m in range(rows // chunk):
            at = slice(m * chunk, (m + 1) * chunk)
            acc[at, :] = jnp.where(step == 0, 0.0, acc[at, :]) + rows_step(r, m)

    @pl.when(step == nt - 1)
    def _():
        load_cot.wait()
        sum_ref[...] = jnp.zeros_like(sum_ref)
        tail = 128
        for m in range(rows // chunk):
            branch = rows_step(nt - 1, m)
            for k in range(0, chunk, tail):
                at = slice(m * chunk + k, m * chunk + k + tail)
                norm_step(at, m * chunk + k, acc[at, :] + branch[k : k + tail])
        store_result.start()
        store_gf.start()

    def gradient(refs):
        at = step - nt
        r = jnp.where(at < nt // 2, 2 * at + 1, 2 * at - nt)
        product[...] = mm(gf[...], hidden[r], 0, 0).astype(BF16)
        lay_rows(order, scal_ref[0], product, [(ref, (0,)) for ref in refs])

    @pl.when((step >= nt) & (step < nt + nt // 2))
    def _():
        gradient(sent_refs)

    @pl.when(step >= nt + nt // 2)
    def _():
        gradient(kept_refs)

    @pl.when(step == 2 * nt - 1)
    def _():
        store_result.wait()
        store_gf.wait()


def ffn_back_kernel(
    nt, order, up_plan, down_plan, counts, scal_ref, gf_ref, nl_ref, vec_ref, dg_ref, n1_hbm, r1_hbm, *rest
):
    up_pieces, down_pieces, rest = rest[: counts[0]], rest[counts[0] : sum(counts)], rest[sum(counts) :]
    count = len(rest) - 13
    sent_refs, kept_refs = rest[: count // 2], rest[count // 2 : count]
    bup_ref, gb_ref, sum_ref = rest[count : count + 3]
    up, down, acc, gp, product, n1, r1, up_sems, down_sems, more = rest[count + 3 :]
    r = pl.program_id(0)
    rows = gf_ref.shape[0]
    width = up.shape[2]
    chunk = rows
    load_n1 = pltpu.make_async_copy(n1_hbm, n1, more.at[0])
    load_r1 = pltpu.make_async_copy(r1_hbm, r1, more.at[1])
    groups = [(down_plan, down_pieces, down, down_sems), (up_plan, up_pieces, up, up_sems)]
    fetch_weights(scal_ref[0], groups, nt, [load_n1, load_r1])
    bup_ref[...] = jnp.zeros_like(bup_ref)

    def rows_step(m):
        at = slice(m * chunk, (m + 1) * chunk)
        low = gf_ref[at, :]
        for n in range(width // 256):
            span = slice(n * 256, (n + 1) * 256)
            grad = mm(low, down[r, :, span]) * dg_ref[0, at, span].astype(F32)
            grad = grad.astype(BF16)
            gp[at, span] = grad
            bup_ref[0, 0:1, span] += jnp.sum(grad.astype(F32), axis=0, keepdims=True)
        return mm(gp[at, :], up[r], 1, 1)

    def norm_step(at, branch):
        grad_first = gf_ref[at, :].astype(F32) + branch
        normed = n1[at, :].astype(F32)
        low = norm_back(normed, r1[at, 0:1], vec_ref[0:1, :], grad_first).astype(BF16)
        gb_ref[at, :] = low
        sum_ref[0:1, :] += jnp.sum(grad_first * normed, axis=0, keepdims=True)
        sum_ref[1:2, :] += jnp.sum(grad_first, axis=0, keepdims=True)
        sum_ref[2:3, :] += jnp.sum(low.astype(F32), axis=0, keepdims=True)

    def weight_step():
        product[...] = mm(nl_ref[...], gp[...], 0, 0).astype(BF16)

    @pl.when(r < nt - 1)
    def _():
        for m in range(rows // chunk):
            at = slice(m * chunk, (m + 1) * chunk)
            acc[at, :] = jnp.where(r == 0, 0.0, acc[at, :]) + rows_step(m)
        weight_step()

    @pl.when(r == nt - 1)
    def _():
        load_n1.wait()
        load_r1.wait()
        sum_ref[...] = jnp.zeros_like(sum_ref)
        tail = 128
        for m in range(rows // chunk):
            branch = rows_step(m)
            for k in range(0, chunk, tail):
                at = slice(m * chunk + k, m * chunk + k + tail)
                norm_step(at, acc[at, :] + branch[k : k + tail])
        weight_step()

    def places(refs):
        out = []
        for ref in refs:
            out += [(ref, (0,))] if len(ref.shape) == 3 else [(ref, (i, 0)) for i in range(ref.shape[0])]
        return out

    @pl.when(lax.rem(r, 2) == 1)
    def _():
        lay_rows(order, scal_ref[0], product, places(sent_refs))

    @pl.when(lax.rem(r, 2) == 0)
    def _():
        lay_rows(order, scal_ref[0], product, places(kept_refs))


def attend_back_kernel(
    nt,
    part,
    plan,
    count,
    scal_ref,
    gb_ref,
    p_ref,
    q_ref,
    kp_ref,
    vp_ref,
    ks_ref,
    bias_ref,
    px0_ref,
    px1_ref,
    x_hbm,
    heads_hbm,
    *rest,
):
    pieces, rest = rest[:count], rest[count:]
    if part == 0:
        dqx_more, back_more, dqx_ref, back_sent_ref, back_kept_ref, sum_ref, sent_hbm, kept_hbm = rest[:8]
    else:
        dqx_ref, back_ref, sum_ref, sent_hbm, kept_hbm = rest[:5]
    w, kst, vst, dq, dk, dv, x, heads, grads, sems, more = rest[-11:]
    step = pl.program_id(0)
    seq = scal_ref[2] ^ 1 ^ step
    pairs, kp2, pair_cols = kst.shape
    kp = kp2 // 2
    held = pairs * pair_cols
    half = nt // 2
    cols = held // half
    load_x = pltpu.make_async_copy(x_hbm, x, more.at[0])
    load_heads = pltpu.make_async_copy(
        heads_hbm.at[:, :, pl.ds(part * held, held)], heads, more.at[1]
    )

    def fetch():
        return piece_copies(plan, scal_ref[0] & 1, pieces, w, sems)

    @pl.when(step == 0)
    def _():
        for copy in fetch():
            copy.start()
        load_x.start()
        load_heads.start()
        sum_ref[...] = jnp.zeros_like(sum_ref)

    split_pairs(kp_ref, kst)
    split_pairs(vp_ref, vst)

    @pl.when(step == 0)
    def _():
        for copy in fetch():
            copy.wait()

    gb = gb_ref[seq]
    grad_heads = mm(gb, w[3], 1, 1).astype(BF16)
    lane = lax.broadcasted_iota(jnp.int32, (kp, pair_cols), 1) < pair_cols // 2
    for pair in range(pairs):
        span = slice(pair * pair_cols, (pair + 1) * pair_cols)
        probs = p_ref[0, pair * kp2 : (pair + 1) * kp2, :]
        grad = grad_heads[:, span]
        grad_probs = mm(vst[pair], grad, 1, 1)
        both = mm(probs, grad)
        dv[step, :, span] = jnp.where(lane, both[:kp], both[kp:]).astype(BF16)
        weighted = probs.astype(F32) * grad_probs
        parts = []
        for side in range(2):
            cut = slice(side * kp, (side + 1) * kp)
            total = jnp.sum(weighted[cut], axis=0, keepdims=True)
            parts.append((weighted[cut] - probs[cut].astype(F32) * total).astype(BF16))
        grad_scores = jnp.concatenate(parts, 0)
        dq[seq, :, span] = (mm(grad_scores, kst[pair], 0, 0) * SCALE).astype(BF16)
        both = mm(grad_scores, q_ref[0, :, span])
        dk[step, :, span] = jnp.where(lane, both[:kp], both[kp:]).astype(BF16)
    dqx = mm(dq[seq], w[0])
    ks = ks_ref[0][:, 0:1]
    sum_ref[0:1, :] += jnp.sum(dq[seq].astype(F32), axis=0, keepdims=True)
    sum_ref[1:2, :] += jnp.sum(dk[step].astype(F32) * ks, axis=0, keepdims=True)
    sum_ref[2:3, :] += jnp.sum(dv[step].astype(F32) * ks, axis=0, keepdims=True)
    back = mm(dk[step], w[1]) + mm(dv[step], w[2])
    low = bias_ref[:, part * held : (part + 1) * held].astype(BF16)
    terms = mm(low, dk[step], 1, 1)[1:2] + mm(low, dv[step], 1, 1)[2:3]
    terms = jnp.concatenate([jnp.broadcast_to(terms, (16, kp)), jnp.zeros((16, back.shape[1] - kp), F32)], 1)
    if part == 0:
        dqx_ref[0] = (gb.astype(F32) + dqx_more[0].astype(F32) + dqx).astype(BF16)

        def put(ref):
            ref[:kp] = (back + back_more[0, :kp].astype(F32)).astype(BF16)
            ref[kp:] = (terms + back_more[0, kp:].astype(F32)).astype(BF16)

        @pl.when(step == 0)
        def _():
            put(back_sent_ref)

        @pl.when(step == 1)
        def _():
            put(back_kept_ref)

    else:
        dqx_ref[0] = dqx.astype(BF16)
        back_ref[0, :kp] = back.astype(BF16)
        back_ref[0, kp:] = terms.astype(BF16)

    @pl.when(step == 1)
    def _():
        def stores(i):
            out = []
            for j in range(half):
                hbm = (sent_hbm if j % 2 else kept_hbm).at[(scal_ref[scal_ref.shape[0] - 1]) ^ i]
                out.append(
                    pltpu.make_async_copy(grads.at[i, pl.ds(j * cols, cols)], hbm, more.at[2 + i * half + j])
                )
            return out

        def flat(ref):
            return ref[...].reshape(ref.shape[0] * ref.shape[1], ref.shape[2])

        px = jnp.concatenate([px1_ref[...], px0_ref[...]], 0)
        load_x.wait()
        load_heads.wait()
        for i, (a, b) in enumerate(((dq, flat(x)), (dk, px), (dv, px), (heads, flat(gb_ref)))):
            grads[i] = mm(flat(a), b, 0, 0).astype(BF16)
            for copy in stores(i):
                copy.start()
        for i in range(4):
            for copy in stores(i):
                copy.wait()


def finish_kernel(scal_ref, x_ref, here_ref, back_kept_ref, back_other_ref, dqx_ref, sums0_ref, sums0_more, sums1_ref, sums2_ref, bup_ref, gi_ref, *rest):
    pack_refs, pack, total = rest[:4], rest[4], rest[5]
    step = pl.program_id(0)
    seq = scal_ref[2] ^ step
    rows, kp = here_ref.shape
    place = scal_ref[1] + lax.broadcasted_iota(jnp.int32, (rows, kp), 0)
    live = place < scal_ref[3 + seq]
    here = here_ref[...]
    masked = jnp.where(live, here, jnp.zeros_like(here))
    back = jnp.where(step == 0, back_kept_ref[...], back_other_ref[...])
    gi_ref[0] = (dqx_ref[0].astype(F32) + mm(masked, back[:kp])).astype(BF16)
    terms = mm(x_ref[0], back[:kp], 1, 1) + back[kp : kp + 1, :kp].astype(F32)
    terms = jnp.where(live, terms, 0.0)

    @pl.when(step == 0)
    def _():
        total[...] = terms

    @pl.when(step == 1)
    def _():
        both = total[...] + terms
        small = 16
        height = pack.shape[0] - small
        width = pack.shape[1]
        groups = width // kp
        for g in range(groups):
            span = slice(g * kp, (g + 1) * kp)
            count = min(height, rows - g * height)
            pack[:count, span] = both[g * height : g * height + count]
            if count < height:
                pack[count:height, span] = jnp.zeros((height - count, kp), F32)
        pieces = [sums1_ref[2:3], sums1_ref[0:2], sums2_ref[2:3], sums2_ref[0:2]]
        pieces.append(jnp.concatenate([sums0_ref[0:3], sums0_more[0:3]], 1))
        pieces += [bup_ref[j, 0:1] for j in range(bup_ref.shape[0])]
        count = sum(p.shape[0] for p in pieces)
        pieces.append(jnp.zeros((small - count, width), F32))
        pack[height:] = jnp.concatenate(pieces, 0)
        part = pack_refs[0].shape[0]
        for e, ref in enumerate(pack_refs):
            place = pl.multiple_of((scal_ref[scal_ref.shape[0] - 1] ^ e) * part, part)
            ref[...] = pack[pl.ds(place, part), :].astype(BF16)


def unpack_kernel(nt, small, scal_ref, *refs):
    parts, (out_ref, sum_ref, qkv_bias_ref, up_bias_ref, held) = refs[:-5], refs[-5:]
    rows, kp = out_ref.shape[0] // nt, out_ref.shape[1]
    part = parts[0].shape[2]
    height = held.shape[0] - small
    for t in range(nt):
        ref = parts[t % 2]
        for e in range(ref.shape[1]):
            place = pl.multiple_of((scal_ref[scal_ref.shape[0] - 1] ^ e) * part, part)
            held[pl.ds(place, part), :] = ref[t // 2, e].astype(F32)
        base = (lax.div(scal_ref[1], rows) ^ t) * rows
        for g in range(held.shape[1] // kp):
            count = min(height, rows - g * height)
            place = pl.multiple_of(base + g * height, 16)
            out_ref[pl.ds(place, count), :] = held[:count, g * kp : (g + 1) * kp]
        rows_here = held[height:, :]
        total = rows_here if t == 0 else total + rows_here
        size = qkv_bias_ref.shape[1]
        mine = rows_here[6:9, t * size : (t + 1) * size]
        qkv_bias = mine if t == 0 else qkv_bias + mine
        mine = rows_here[9 + t : 10 + t, :]
        up_bias = mine if t == 0 else up_bias + mine
    sum_ref[...] = total[:8]
    qkv_bias_ref[...] = qkv_bias
    up_bias_ref[...] = up_bias


def settle_kernel(scal_ref, *refs):
    parts, (qkv_ref, out_ref, held) = refs[:-3], refs[-3:]
    for e, ref in enumerate(parts):
        held[scal_ref[scal_ref.shape[0] - 1] ^ e] = ref[...].astype(F32)
    qkv_ref[...] = held[:3]
    out_ref[...] = held[3]


def whole(shape, buffers=None):
    mode = {} if buffers is None else {"pipeline_mode": pl.Buffered(buffers)}
    return pl.BlockSpec(shape, lambda *ids: (0,) * len(shape), **mode)


def call(kernel, name, grid, in_specs, out_specs, out_shapes, scratch, flops, moved, args):
    return pl.pallas_call(
        kernel,
        grid_spec=pltpu.PrefetchScalarGridSpec(
            num_scalar_prefetch=1, grid=grid, in_specs=in_specs, out_specs=out_specs, scratch_shapes=scratch
        ),
        out_shape=[jax.ShapeDtypeStruct(*s) for s in out_shapes],
        compiler_params=pltpu.CompilerParams(vmem_limit_bytes=VMEM_BYTES),
        cost_estimate=pl.CostEstimate(flops=flops, bytes_accessed=moved, transcendentals=0),
        name=name,
    )(*args)


ANY = pl.BlockSpec(memory_space=pl.ANY)


def project(scalars, x, length_proj):
    seqs, rows, width = x.shape
    kp = length_proj.shape[1]
    return call(
        functools.partial(project_kernel, seqs),
        "project",
        (seqs,),
        [
            pl.BlockSpec((1, rows, width), lambda i, s: (s[2] ^ 1 ^ i, 0, 0)),
            pl.BlockSpec((rows, kp), lambda i, s: (lax.div(s[1], rows), 0)),
            whole(length_proj.shape),
        ],
        [
            whole((kp, width)),
            whole((kp, width)),
            pl.BlockSpec((1, kp, 128), lambda i, s: (s[2] ^ 1 ^ i, 0, 0)),
        ],
        [((kp, width), BF16), ((kp, width), F32), ((seqs, kp, 128), F32)],
        [],
        1_000_000_000,
        5_000_000,
        (scalars, x, length_proj, length_proj),
    )


def attend(scalars, x, px0, px1, key_sum, plan, pieces, biases, vectors):
    seqs, rows, width = x.shape
    kp = px0.shape[0]
    pairs = width // (2 * DH)
    by_seq = lambda i, s: (s[2] ^ i, 0, 0)
    outs = [
        (rows, width, BF16),
        (2 * pairs * kp, rows, BF16),
        (kp, width, BF16),
        (kp, width, BF16),
        (rows, width, BF16),
        (rows, width, BF16),
        (rows, width, BF16),
        (rows, 128, F32),
    ]
    return call(
        functools.partial(attend_kernel, plan, len(pieces)),
        "attend",
        (seqs,),
        [
            pl.BlockSpec((1, rows, width), by_seq),
            whole(px0.shape),
            whole(px1.shape),
            pl.BlockSpec((1, kp, 128), by_seq),
        ]
        + [ANY] * len(pieces)
        + [whole(biases.shape), whole(vectors.shape)],
        [pl.BlockSpec((1, r, c), by_seq) for r, c, _ in outs],
        [((seqs, r, c), t) for r, c, t in outs],
        [
            pltpu.VMEM((4, width, width), BF16),
            pltpu.VMEM((pairs, 2 * kp, 2 * DH), BF16),
            pltpu.VMEM((pairs, 2 * kp, 2 * DH), BF16),
            pltpu.SemaphoreType.DMA((len(plan),)),
        ],
        14_000_000_000,
        25_000_000,
        (scalars, x, px0, px1, key_sum, *pieces, biases, vectors),
    )


def ffn(order, parts, scalars, nl, vectors, biases, cotangent, up, down, seq_rows):
    rows, width = nl.shape
    nt, _, hidden = biases.shape
    half = nt // 2
    (up_plan, up_pieces), (down_plan, down_pieces) = up, down
    counts = (len(up_pieces), len(down_pieces))
    rows_in = width
    part = width // parts
    return call(
        functools.partial(ffn_kernel, nt, order, up_plan, down_plan, counts, seq_rows),
        "feed_forward",
        (2 * nt,),
        [whole((rows, width), 1), whole(vectors.shape), whole(biases.shape), ANY] + [ANY] * sum(counts),
        [
            pl.BlockSpec((1, rows, hidden), lambda i, s: (jnp.minimum(i, nt - 1), 0, 0)),
            *[pl.BlockSpec((1, part, hidden), lambda i, s: (jnp.clip(i - nt, 0, half - 1), 0, 0))] * parts,
            *[pl.BlockSpec((1, part, hidden), lambda i, s: (jnp.clip(i - nt - half, 0, half - 1), 0, 0))] * parts,
            whole((8, width)),
            ANY,
            ANY,
        ],
        [
            ((nt, rows, hidden), BF16),
            *[((half, part, hidden), BF16)] * (2 * parts),
            ((8, width), F32),
            ((rows, width), BF16),
            ((rows, width), BF16),
        ],
        [
            pltpu.VMEM((nt, rows_in, hidden), BF16),
            pltpu.VMEM((nt, rows_in, hidden), BF16),
            pltpu.VMEM((nt, rows, hidden), BF16),
            pltpu.VMEM((rows, width), F32),
            pltpu.VMEM((rows, width), BF16),
            pltpu.VMEM((rows, width), BF16),
            pltpu.VMEM((rows, width), BF16),
            pltpu.VMEM((rows_in, hidden), BF16),
            pltpu.SemaphoreType.DMA((len(up_plan),)),
            pltpu.SemaphoreType.DMA((len(down_plan),)),
            pltpu.SemaphoreType.DMA((3,)),
        ],
        24_000_000_000,
        30_000_000,
        (scalars, nl, vectors, biases, cotangent, *up_pieces, *down_pieces),
    )


def ffn_back(order, parts, scalars, gf, nl, vectors, slopes, n1, r1, up, down):
    rows, width = n1.shape
    nt, _, hidden = slopes.shape
    half = nt // 2
    part = width // parts
    (up_plan, up_pieces), (down_plan, down_pieces) = up, down
    counts = (len(up_pieces), len(down_pieces))
    by_chip = [pl.BlockSpec((1, part, hidden), lambda i, s: (lax.div(i, 2), 0, 0))]
    chip_shapes = [((half, part, hidden), BF16)]
    if parts > 1:
        by_chip.append(pl.BlockSpec((parts - 1, 1, part, hidden), lambda i, s: (0, lax.div(i, 2), 0, 0)))
        chip_shapes.append(((parts - 1, half, part, hidden), BF16))
    return call(
        functools.partial(ffn_back_kernel, nt, order, up_plan, down_plan, counts),
        "feed_forward_back",
        (nt,),
        [
            whole((rows, width), 1),
            whole((rows, width), 1),
            whole(vectors.shape),
            pl.BlockSpec((1, rows, hidden), lambda i, s: (i, 0, 0)),
            ANY,
            ANY,
        ]
        + [ANY] * sum(counts),
        [
            *by_chip,
            *by_chip,
            pl.BlockSpec((1, 8, hidden), lambda i, s: (i, 0, 0)),
            whole((rows, width)),
            whole((8, width)),
        ],
        [
            *chip_shapes,
            *chip_shapes,
            ((nt, 8, hidden), F32),
            ((rows, width), BF16),
            ((8, width), F32),
        ],
        [
            pltpu.VMEM((nt, width, hidden), BF16),
            pltpu.VMEM((nt, width, hidden), BF16),
            pltpu.VMEM((rows, width), F32),
            pltpu.VMEM((rows, hidden), BF16),
            pltpu.VMEM((width, hidden), BF16),
            pltpu.VMEM((rows, width), BF16),
            pltpu.VMEM((rows, 128), F32),
            pltpu.SemaphoreType.DMA((len(up_plan),)),
            pltpu.SemaphoreType.DMA((len(down_plan),)),
            pltpu.SemaphoreType.DMA((2,)),
        ],
        24_000_000_000,
        25_000_000,
        (scalars, gf, nl, vectors, slopes, n1, r1, *up_pieces, *down_pieces),
    )


def attend_back(nt, part, scalars, gb, probs, q, kproj, vproj, key_sum, biases, px0, px1, x, heads, plan, pieces, more):
    seqs, rows, width = gb.shape
    kp = kproj.shape[1]
    half = nt // 2
    cols = width // nt
    pairs = width // (4 * DH)
    held = width // 2
    plan = [(p, row, block - 2 * part, kind, turned) for p, row, block, kind, turned in plan if block // 2 == part]
    by_seq = lambda i, s: (s[2] ^ 1 ^ i, 0, 0)
    by_part = lambda i, s: (s[2] ^ 1 ^ i, 0, part)
    rows_block = pl.BlockSpec((1, rows, width), by_seq)
    back_block = pl.BlockSpec((1, kp + 16, width), by_seq)
    back_specs = [back_block] if part else [whole((kp + 16, width)), whole((kp + 16, width))]
    back_shapes = [((seqs, kp + 16, width), BF16)] if part else [((kp + 16, width), BF16)] * 2
    return call(
        functools.partial(attend_back_kernel, nt, part, plan, len(pieces)),
        "attend_back",
        (seqs,),
        [
            whole(gb.shape, 1),
            pl.BlockSpec((1, 2 * pairs * kp, rows), lambda i, s: (s[2] ^ 1 ^ i, part, 0)),
            pl.BlockSpec((1, rows, held), by_part),
            pl.BlockSpec((1, kp, held), by_part),
            pl.BlockSpec((1, kp, held), by_part),
            pl.BlockSpec((1, kp, 128), by_seq),
            whole(biases.shape),
            whole(px0.shape),
            whole(px1.shape),
            ANY,
            ANY,
        ]
        + [ANY] * len(pieces)
        + ([] if part else [rows_block, back_block]),
        [rows_block, *back_specs, whole((8, held)), ANY, ANY],
        [
            ((seqs, rows, width), BF16),
            *back_shapes,
            ((8, held), F32),
            ((4, cols, width), BF16),
            ((4, cols, width), BF16),
        ],
        [
            pltpu.VMEM((4, held, width), BF16),
            pltpu.VMEM((pairs, 2 * kp, 2 * DH), BF16),
            pltpu.VMEM((pairs, 2 * kp, 2 * DH), BF16),
            pltpu.VMEM((seqs, rows, held), BF16),
            pltpu.VMEM((seqs, kp, held), BF16),
            pltpu.VMEM((seqs, kp, held), BF16),
            pltpu.VMEM((seqs, rows, width), BF16),
            pltpu.VMEM((seqs, rows, held), BF16),
            pltpu.VMEM((4, held, width), BF16),
            pltpu.SemaphoreType.DMA((len(plan),)),
            pltpu.SemaphoreType.DMA((2 + 4 * half,)),
        ],
        10_000_000_000,
        18_000_000,
        (scalars, gb, probs, q, kproj, vproj, key_sum, biases, px0, px1, x, heads, *pieces, *more),
    )


def finish(scalars, x, length_proj, back_kept, back_other, dqx, sums0, sums0_more, sums1, sums2, bup, pack_rows):
    seqs, rows, width = x.shape
    kp = length_proj.shape[1]
    by_seq = lambda i, s: (s[2] ^ i, 0, 0)
    return call(
        finish_kernel,
        "finish",
        (seqs,),
        [
            pl.BlockSpec((1, rows, width), by_seq),
            pl.BlockSpec((rows, kp), lambda i, s: (lax.div(s[1], rows), 0)),
            whole(back_kept.shape),
            whole(back_other.shape),
            pl.BlockSpec((1, rows, width), by_seq),
            whole(sums0.shape),
            whole(sums0_more.shape),
            whole(sums1.shape),
            whole(sums2.shape),
            whole(bup.shape),
        ],
        [pl.BlockSpec((1, rows, width), by_seq), *[whole((pack_rows // 4, width))] * 4],
        [((seqs, rows, width), BF16), *[((pack_rows // 4, width), BF16)] * 4],
        [pltpu.VMEM((pack_rows, width), F32), pltpu.VMEM((rows, kp), F32)],
        2_000_000_000,
        6_000_000,
        (scalars, x, length_proj, back_kept, back_other, dqx, sums0, sums0_more, sums1, sums2, bup),
    )


def unpack(scalars, parts, rows, kp, small):
    chips, quarters, part, width = parts[0].shape
    nt = chips * len(parts)
    return call(
        functools.partial(unpack_kernel, nt, small),
        "unpack",
        (),
        [whole(p.shape) for p in parts],
        [whole((nt * rows, kp)), whole((8, width)), whole((3, width // nt)), whole((1, width))],
        [((nt * rows, kp), F32), ((8, width), F32), ((3, width // nt), F32), ((1, width), F32)],
        [pltpu.VMEM((quarters * part, width), F32)],
        1_000_000,
        4_000_000,
        (scalars, *parts),
    )


def settle(scalars, parts):
    rows, width = parts[0].shape
    return call(
        settle_kernel,
        "settle",
        (),
        [whole(p.shape) for p in parts],
        [whole((3, rows, width)), whole((rows, width))],
        [((3, rows, width), F32), ((rows, width), F32)],
        [pltpu.VMEM((4, rows, width), F32)],
        1_000_000,
        4_000_000,
        (scalars, *parts),
    )


def local(
    dp,
    tp,
    inputs,
    lengths,
    w_qkv,
    b_qkv,
    output_weight,
    b_out,
    length_proj,
    first_gain,
    first_shift,
    w_up,
    hidden_bias,
    w_down,
    b_down,
    second_gain,
    second_shift,
    cotangent,
):
    seqs, local_len, width = inputs.shape
    cols = w_qkv.shape[2]
    kp = length_proj.shape[1]
    hidden_cols = w_up.shape[1]
    block_rows = w_up.shape[0]
    tbits, dbits = bits_of(tp), bits_of(dp)
    t_index = lax.axis_index("tensor")
    rows_count = seqs * local_len
    relative = block_rows % 16 == 0 and (tp, dp) == (4, 8)

    dp_index = lax.axis_index("dp")
    if relative:
        y, z, zz = dbits
        square_xy = [0, zz, z, z ^ zz]
        square_xy = square_xy + [o ^ y for o in square_xy]
        square_yz = [o ^ zz * half for o in (y ^ z, 0, y, z) for half in range(2)]
    else:
        square_xy = square_yz = [0]
        dp_index = jnp.zeros((), jnp.int32)
    where = jnp.stack([dp_index, t_index * local_len, t_index & 1]).astype(jnp.int32)
    quarter = (lax.axis_index("dp") & 3).astype(jnp.int32)
    scalars = jnp.concatenate([where, lengths.astype(jnp.int32), quarter[None]])
    vectors = jnp.stack(
        [first_gain, first_shift, b_down, second_gain, second_shift, b_out, b_out, b_out]
    )

    core, chip = tbits

    def over_core(value):
        return swap(value, "tensor", core, tp)

    def over_chip(value):
        return swap(value, "tensor", chip, tp)

    def over_dp(value, bit):
        return swap(value, "dp", bit, dp)

    line = Line()

    if relative:
        a_far, m_far = over_dp(w_up, zz), over_dp(w_down, zz)
    qkv_rows = w_qkv.transpose(1, 2, 0)
    halves = jnp.where(own_bit("dp", 1), jnp.stack([qkv_rows[2], output_weight]), qkv_rows[:2])
    first = over_chip(halves.reshape(2 * cols, width))
    bias_rows = jnp.zeros((8, width), F32)
    bias_rows = bias_rows.at[0:3, :cols].set(b_qkv).at[3, :hidden_cols].set(hidden_bias)
    bias_chip = over_chip(bias_rows)

    def plan_of(pieces, blocks):
        rows = sum(p.shape[0] for p in pieces) // sum(len(b) for b in blocks)
        plan = [(i, k * rows, r, rel) for i, b in enumerate(blocks) for k, (r, rel) in enumerate(b)]
        plan += [(i + len(pieces), row, r + 1, rel) for i, row, r, rel in plan]
        return plan, pieces + [over_core(p) for p in pieces]

    sent, kept, key_sum = project(scalars, inputs, length_proj)
    if relative:
        sent, kept, a_far = line.meet(sent, kept, a_far)
        a = jnp.concatenate([w_up, a_far], 0)
        ay = over_dp(a, y)
    else:
        sent, kept = line.meet(sent, kept)
    px0 = add(kept, line.meet(over_core(sent)))
    px_chip = over_chip(px0)
    if relative:
        ay = line.meet(ay)
        a = jnp.concatenate([a, ay], 0)
        az, ax = over_dp(a, z), over_chip(a)
    first, bias_chip = line.meet(first, bias_chip)
    second = over_dp(first, 1)
    bias_all = jnp.stack([bias_rows, over_core(bias_rows), bias_chip, over_core(bias_chip)])
    biases = jnp.pad(bias_all[:, :3, :cols].transpose(1, 0, 2).reshape(3, tp * cols), ((0, 5), (0, 0)))
    bias_hidden = bias_all[:, 3:4, :hidden_cols]
    if relative:
        m_far = line.meet(m_far)
        m = jnp.concatenate([w_down, m_far], 0)
        m_chip = over_chip(m)
    px_chip = line.meet(px_chip)
    px0 = add(px0, px_chip)
    px1 = over_core(px0)
    if relative:
        m_chip = line.meet(m_chip)
        m = jnp.concatenate([m, m_chip], 0)
        my, mz = over_dp(m, y), over_dp(m, z)
    second = line.meet(second)
    pieces = [qkv_rows.reshape(3 * cols, width), output_weight, first, second]
    pieces = pieces + [over_core(p) for p in pieces]
    plan = [(0, i * cols, 0, i, False) for i in range(3)] + [(1, 0, 0, 3, False)]
    plan += [(2, i * cols, 2, i, True) for i in range(2)] + [(3, i * cols, 2, i ^ 2, True) for i in range(2)]
    plan += [(p + 4, row, block + 1, kind, turned) for p, row, block, kind, turned in plan]
    if relative:
        az = line.meet(az)
        axz = over_chip(az)
        my = line.meet(my)
        myz = over_dp(my, z)
    biases, bias_hidden, vectors = line.meet(biases, bias_hidden, vectors)

    q, probs, kproj, vproj, heads, n1, nl, r1 = attend(
        scalars, line.after(inputs), px0, px1, key_sum, plan, pieces, biases, vectors
    )
    nl, n1, r1 = (v.reshape(rows_count, -1) for v in (nl, n1, r1))
    if relative:
        nl, ax, mz, axz, myz = line.meet(nl, ax, mz, axz, myz)
        orders = [[0, zz, y, y ^ zz], [z, z ^ zz, y ^ z, y ^ z ^ zz]]
        up = plan_of([a, az, ax, axz], [[(r, o) for o in half] for r in (0, 2) for half in orders])
        blocks = [[(r, o ^ e) for r in (0, 2) for e in (0, zz)] for o in (0, y, z, y ^ z)]
        down = plan_of([m, my, mz, myz], blocks)
    else:
        nl = line.meet(nl)
        pieces_up, pieces_down = (lax.all_gather(w, "dp", axis=0, tiled=True) for w in (w_up, w_down))
        up = plan_of([pieces_up, over_chip(pieces_up)], [[(0, 0)], [(2, 0)]])
        down = plan_of([pieces_down, over_chip(pieces_down)], [[(0, 0)], [(2, 0)]])
    parts = 2 if relative else 1
    outs = ffn(
        square_xy,
        parts,
        scalars,
        nl,
        vectors,
        bias_hidden,
        cotangent.reshape(rows_count, width),
        up,
        down,
        local_len,
    )
    slopes, down_sent, down_kept = outs[0], outs[1 : 1 + parts], outs[1 + parts : 1 + 2 * parts]
    sums2, result, gf = outs[1 + 2 * parts :]

    def scatter_plain(kept, got):
        value = add(kept, got)
        value = add(value[0], over_chip(value[1])).astype(F32)
        return lax.psum_scatter(value, "dp", scatter_dimension=0, tiled=True)

    if relative:
        got_b, got_a = over_core(down_sent[1]), over_core(down_sent[0])
        gf, got_b = line.meet(gf, got_b)
        b1 = add(down_kept[1][1], got_b[1])
        got_b1 = over_dp(b1, y)
        gf, b1 = line.meet(gf, b1)
    else:
        got_down = over_core(down_sent[0])
        gf = line.meet(gf)
    outs = ffn_back(
        square_yz, 4 if relative else 1, scalars, line.after(gf), nl, vectors, slopes, n1, r1, up, down
    )
    bup, gb, sums1 = outs[-3:]
    if relative:
        up_sent, up_sent_more, up_kept, up_kept_more = outs[:4]
        gb, up_sent, got_a, got_b1 = line.meet(gb, up_sent, got_a, got_b1)
        a1 = add(down_kept[0][1], got_a[1], got_b1)
        b = add(down_kept[1][0], got_b[0])
        got_a1, got_b = over_chip(a1), over_dp(b, y)
        got_up, got_up_more = over_core(up_sent), over_core(up_sent_more)
        got_up = line.meet(got_up)
        myz = add(up_kept, got_up)
        got_myz = over_dp(myz, z)
        gb, myz = line.meet(gb, myz)
    else:
        up_sent, up_kept = outs[:2]
        got_up = over_core(up_sent)
        down_weight_gradient = scatter_plain(down_kept[0], got_down)
        up_weight_gradient = scatter_plain(up_kept, got_up)
        gb = line.meet(gb)

    def heads_back(part, more):
        return attend_back(
            tp,
            part,
            scalars,
            line.after(gb).reshape(seqs, local_len, width),
            probs,
            q,
            kproj,
            vproj,
            key_sum,
            biases,
            px0,
            px1,
            inputs,
            heads,
            plan,
            pieces,
            more,
        )

    dqx, back, sums0_more, sent1, kept1 = heads_back(1, [])
    if relative:
        sent1, kept1, got_a1, got_b, got_myz, got_up_more = line.meet(
            sent1, kept1, got_a1, got_b, got_myz, got_up_more
        )
        near_rows, far_rows = slice(0, 2 * block_rows), slice(2 * block_rows, None)
        a, a_sent = (
            add(down_kept[0][0, at], got_a[0, at], got_a1[at], got_b[at]) for at in (near_rows, far_rows)
        )
        got_a = over_dp(a_sent, z)
    else:
        sent1, kept1 = line.meet(sent1, kept1)
    got1 = line.meet(over_core(sent1))
    near, further = dbits[:2], dbits[2:]
    corners = [0, near[0], near[1], near[0] ^ near[1]]

    def to_corners(parts):
        return [over_dp(part, corner) for part, corner in zip(parts, corners[1:])]

    attn1 = line.meet(*[add(kept1[e], got1[e]) for e in range(4)])
    got_attn1 = to_corners(attn1[1:])
    dqx, back_sent, back_kept, sums0, sent0, kept0 = heads_back(0, [dqx, back])

    if relative:
        back_sent, back_kept, sent0, kept0, got_a, *got_attn1 = line.meet(
            back_sent, back_kept, sent0, kept0, got_a, *got_attn1
        )
    else:
        back_sent, back_kept, sent0, kept0, *got_attn1 = line.meet(
            back_sent, back_kept, sent0, kept0, *got_attn1
        )
    got_back, got0 = over_core(back_sent), over_core(sent0)
    if relative:
        a, a_sent = (add(a[at], got_a[at]) for at in (slice(0, block_rows), slice(block_rows, None)))
        got_a = over_dp(a_sent, zz)
    back_kept = add(back_kept, line.meet(got_back))
    got_back = over_chip(back_kept)
    got0 = line.meet(got0)
    attn = [add(kept0[e], got0[e]) for e in range(4)]
    got_attn = to_corners(attn[1:])
    attn1 = add_pairs(attn1[0], *got_attn1)
    got_attn1 = over_chip(attn1)
    if relative:
        got_back, got_attn[0], got_attn[1], got_a = line.meet(got_back, got_attn[0], got_attn[1], got_a)
        down_weight_gradient = a.astype(F32) + got_a.astype(F32)
    else:
        got_back, got_attn[0], got_attn[1] = line.meet(got_back, got_attn[0], got_attn[1])
    back_kept = add(back_kept, got_back)
    back_other = line.meet(over_core(back_kept))

    def over_rest(value):
        for bit in further[1:]:
            value = add(value, over_dp(value, bit))
        return value

    small = 16
    height = -(-local_len * kp // width // 16) * 16
    grad_inputs, *shared = finish(
        scalars,
        inputs,
        length_proj,
        back_kept,
        back_other,
        dqx,
        sums0,
        sums0_more,
        sums1,
        sums2,
        bup,
        height + small,
    )
    met = line.meet(*shared, *got_attn, got_attn1)
    shared, got_attn, got_attn1 = met[:4], met[4:7], met[7]
    attn = add(add_pairs(attn[0], *got_attn), got_attn1)
    attn, *shared = line.meet(attn, *shared)
    if relative:
        my, mz = add(up_kept_more[1], got_up_more[1], got_myz), add(up_kept_more[2], got_up_more[2])
        my, mz = line.meet(my, mz)
        got_my, got_mz = over_dp(my, y), over_dp(mz, z)
    got = over_dp(attn, further[0])
    got_shared = line.meet(*to_corners(shared[1:]))
    shared = add_pairs(shared[0], *got_shared)
    got_more = over_dp(shared, further[0])
    got, got_more = line.meet(got, got_more)
    attn, shared = over_rest(add(attn, got)), over_rest(add(shared, got_more))
    got_attn = to_corners([attn] * 3)
    got_shared, got_attn[0] = line.meet(over_chip(shared), got_attn[0])
    shared = jnp.stack([shared, got_shared])
    if relative:
        got_my, got_mz = line.meet(got_my, got_mz)
        m, m_sent = (add(up_kept_more[0][c], got_up_more[0][c], got_my[c], got_mz[c]) for c in range(2))
        got_m = over_chip(m_sent)
    *got_shared, got_attn[1], got_attn[2] = line.meet(*to_corners([shared] * 3), *got_attn[1:])
    shared = jnp.stack([shared, *got_shared], 1)
    got_shared = over_core(shared)
    grad_w_qkv, grad_w_out = settle(scalars, [attn, *got_attn])
    grad_w_qkv = grad_w_qkv.transpose(2, 0, 1)
    if relative:
        m = add(m, line.meet(got_m))
        got_m = over_dp(m[block_rows:], zz)
    grad_length_proj, sums, grad_b_qkv, grad_b_up = unpack(
        scalars, [shared, line.meet(got_shared)], local_len, kp, small
    )
    if relative:
        up_weight_gradient = m[:block_rows].astype(F32) + line.meet(got_m).astype(F32)
    whole_sum = [sums[i] for i in range(6)]
    grad_b_up = grad_b_up[0, :hidden_cols]

    shape = (seqs, local_len, width)
    return (
        result.reshape(shape),
        grad_inputs,
        grad_w_qkv,
        grad_b_qkv,
        grad_w_out,
        whole_sum[0],
        grad_length_proj,
        whole_sum[1],
        whole_sum[2],
        up_weight_gradient,
        grad_b_up,
        down_weight_gradient,
        whole_sum[3],
        whole_sum[4],
        whole_sum[5],
    )


def solution(mesh):
    placed = (
        P("dp", "tensor", None),
        P("dp"),
        P(None, None, "tensor"),
        P(None, "tensor"),
        P("tensor", None),
        P(),
        P(),
        P(),
        P(),
        P("dp", "tensor"),
        P("tensor"),
        P("dp", "tensor"),
        P(),
        P(),
        P(),
        P("dp", "tensor", None),
    )
    return jax.shard_map(
        functools.partial(local, mesh.shape["dp"], mesh.shape["tensor"]),
        mesh=mesh,
        in_specs=placed,
        out_specs=(
            P("dp", "tensor", None),
            P("dp", "tensor", None),
            P(None, None, "tensor"),
            P(None, "tensor"),
            P("tensor", None),
            P(),
            P(),
            P(),
            P(),
            P("dp", "tensor"),
            P("tensor"),
            P("dp", "tensor"),
            P(),
            P(),
            P(),
        ),
        check_vma=False,
    )
```
